32 devices in a mesh: groups: 2 (over y), level: 4 (over z), src: 2 (over x), phase: 2 (over core).
Axes of the slice: x: 2, y: 2, z: 4, core: 2. Of those that a mesh axis runs over, the one named last changes fastest.
Arguments:
- state_values: float32 [24, 8, 32, 16, 128], P(('groups', 'level'), 'src', 'phase'), parts along dimension 0, may hold values from -6 to 6
- phase_rates: float32 [64, 32], P('groups'), parts along dimension 0, may hold values from 0.05 to 2
- batch_rates: float32 [32, 32, 32], P('groups'), parts along dimension 0, may hold values from 0.02 to 1
- service_rates: float32 [4], P('groups'), parts along dimension 0, may hold values from 20 to 60
- source_rates: float32 [6, 3], P('groups'), parts along dimension 0, may hold values from 2 to 30
- tile_levels: int32 [16, 2], P('groups'), parts along dimension 0, may hold values from 0 to 3, as said below
- routes: int32 [16, 5], P('groups'), parts along dimension 0, may hold values from -1 to 7, as said below
- tile_owner: int32 [16], P('groups'), parts along dimension 0, may hold values from 0 to 11, as said below
Outputs:
- stepped_values: float32 [24, 8, 32, 16, 128], P(('groups', 'level'), 'src', 'phase'), parts along dimension 0
The draws below stay inside these ranges and needn't reach their ends.
There are 2 independent parts, one for each index of `groups`. The reference program is written for one: setup_inputs(seed, part) draws one part's arguments, and reference() takes and returns one part's arrays. A program takes and returns all parts, laid end to end along the dimension named above; each array names one. Nothing has to cross between parts.
Inputs may be any that keep to these rules, and one draw needn't show every extreme that they name: `tile_levels`: row t is the tile (a, c) covering buffer-one levels a * 128 to a * 128 + 127 and buffer-two levels c * 16 to c * 16 + 15; tiles are numbered column by column (c rising, then a rising), every c from 0 to 3 has tiles a = 0, 1, ... up to its own height, and the tallest column has 3 tiles. routes[t] lists the tiles (a - 1, c), (a + 1, c), (a, c - 1), (a, c + 1) and (a + 1, c - 1) of tile t = (a, c), or -1 where no such tile exists. `tile_owner`: each tile has its own slot; slots d * 3 to d * 3 + 2 belong to index d of level. Every index holds 1 to 3 tiles, the busiest exactly 3, with consecutive tile numbers in its first slots in order. Slots that hold no tile are ignored.
All inputs are finite; a program needn't handle non-finite values.
Results may differ from the reference program's by a relative error of at most 0.0001.
Values sent between devices are 32-bit elements; how exact they have to be, the bound alone decides.
A program may use at most 128 MiB of HBM per device.

```python
import math
import jax
import jax.numpy as jnp
from jax import lax

P_SIZE = 32
BATCH = 16
SOURCES = 3
STATES = 8
TB1 = 128
TB2 = 16
MEAN_TILES = 2
CAP = 3
TILES = 8
COLS = 4
SLOTS = 12
N_LEVEL = 4


def pair_counts(key, groups, mean_size):
    perm_key, spread_key = jax.random.split(key)
    shuffled = jax.random.permutation(perm_key, groups)
    spread = jax.random.randint(spread_key, (groups // 2,), 0, mean_size)
    spread = spread.at[0].set(mean_size - 1)
    values = jnp.concatenate([mean_size + spread, mean_size - spread]).astype(jnp.int32)
    return jnp.zeros((groups,), jnp.int32).at[shuffled].set(values)


def tile_layout(key):
    base_key = jax.random.fold_in(key, 5)
    cols_key, devs_key, shuffle_key = jax.random.split(base_key, 3)
    heights = pair_counts(cols_key, COLS, MEAN_TILES)
    counts = pair_counts(devs_key, N_LEVEL, MEAN_TILES)
    device_order = jax.random.permutation(shuffle_key, N_LEVEL).astype(jnp.int32)
    busiest = jnp.argmax(counts).astype(jnp.int32)
    last_at = jnp.argmax(device_order == N_LEVEL - 1).astype(jnp.int32)
    moved_device = device_order[busiest]
    device_order = device_order.at[last_at].set(moved_device).at[busiest].set(N_LEVEL - 1).astype(jnp.int32)
    tile_ids = jnp.arange(TILES, dtype=jnp.int32)
    column_end = jnp.cumsum(heights).astype(jnp.int32)
    column_start = column_end - heights
    column = jnp.sum((column_end[None, :] <= tile_ids[:, None]).astype(jnp.int32), axis=1).astype(jnp.int32)
    tier_pos = tile_ids - column_start[column]
    height_here = heights[column]
    left_col = jnp.maximum(column - 1, 0)
    right_col = jnp.minimum(column + 1, COLS - 1)
    from_below = jnp.where(tier_pos > 0, tile_ids - 1, -1)
    from_above = jnp.where(tier_pos + 1 < height_here, tile_ids + 1, -1)
    from_left = jnp.where((column > 0) & (tier_pos < heights[left_col]), column_start[left_col] + tier_pos, -1)
    from_right = jnp.where((column + 1 < COLS) & (tier_pos < heights[right_col]), column_start[right_col] + tier_pos, -1)
    corner = jnp.where((column > 0) & (tier_pos + 1 < heights[left_col]), column_start[left_col] + tier_pos + 1, -1)
    routes = jnp.stack([from_below, from_above, from_left, from_right, corner], axis=1).astype(jnp.int32)
    range_end = jnp.cumsum(counts).astype(jnp.int32)
    range_start = range_end - counts
    holder = jnp.sum((range_end[None, :] <= tile_ids[:, None]).astype(jnp.int32), axis=1).astype(jnp.int32)
    owner = (device_order[holder] * CAP + tile_ids - range_start[holder]).astype(jnp.int32)
    levels = jnp.stack([tier_pos, column], axis=1).astype(jnp.int32)
    return (levels, routes, owner)


def draw_tile_levels(key, part):
    return tile_layout(key)[0]


def draw_routes(key, part):
    return tile_layout(key)[1]


def draw_tile_owner(key, part):
    return tile_layout(key)[2]


def level_of(key, extent, shards, least, top_value):
    def one(position, shards_of):
        steps = jax.random.uniform(jax.random.fold_in(jax.random.fold_in(key, 6), position), (shards_of,), jnp.float32, least / len(shards), top_value / len(shards))
        return jnp.repeat(jnp.exp(steps), extent[position] // shards_of).reshape((-1,) + (1,) * (len(extent) - position - 1))

    level = one(*shards[0])
    for cut in shards[1:]:
        level = level * one(*cut)
    return level


def normal_values(rng, extent, scale, limit, pieces=(), held_as=jnp.bfloat16):
    values = scale * jax.random.normal(rng, extent, jnp.float32)
    if pieces:
        values = values * level_of(rng, extent, pieces, -0.22, 0.18)
    return jnp.clip(values, -limit, limit).astype(held_as)


def setup_inputs(seed: int = 0, part: int = 0) -> dict:
    seeds = jax.random.split(jax.random.key(seed), 9)
    own_keys = jax.random.split(jax.random.fold_in(seeds[8], part), 9)
    return {
        "state_values": normal_values(own_keys[0], (SLOTS, STATES, P_SIZE, TB2, TB1), 1.0, 6.0, ((0, 4), (1, 2), (2, 2)), jnp.float32),
        "phase_rates": jnp.clip(jnp.exp(jax.random.uniform(own_keys[1], (P_SIZE, P_SIZE), jnp.float32, math.log(0.05), math.log(2.0))), 0.05, 2.0),
        "batch_rates": jnp.clip(jnp.exp(jax.random.uniform(own_keys[2], (BATCH, P_SIZE, P_SIZE), jnp.float32, math.log(0.02), math.log(1.0))), 0.02, 1.0),
        "service_rates": jnp.clip(jnp.exp(jax.random.uniform(own_keys[3], (2,), jnp.float32, math.log(20.0), math.log(60.0))), 20.0, 60.0),
        "source_rates": jnp.clip(jnp.exp(jax.random.uniform(own_keys[4], (SOURCES, 3), jnp.float32, math.log(2.0), math.log(30.0))), 2.0, 30.0),
        "tile_levels": draw_tile_levels(jax.random.fold_in(jax.random.fold_in(seeds[8], part), 71), part),
        "routes": draw_routes(jax.random.fold_in(jax.random.fold_in(seeds[8], part), 71), part),
        "tile_owner": draw_tile_owner(jax.random.fold_in(jax.random.fold_in(seeds[8], part), 71), part),
    }


PRECISE = lax.Precision.HIGHEST


def phase_tables(phase_rates, batch_rates):
    phases = phase_rates.shape[0]
    unit_matrix = jnp.eye(phases, dtype=phase_rates.dtype)
    moving = phase_rates * (1.0 - unit_matrix)
    leaving = jnp.sum(moving, axis=1) + jnp.sum(batch_rates, axis=(0, 2))
    stacked = jnp.concatenate([(moving - unit_matrix * leaving[:, None])[None], batch_rates], axis=0)
    return stacked, jnp.max(leaving)


def uniform_rate(top_leaving, service_rates, source_rates):
    sources_top = jnp.sum(jnp.maximum(source_rates[:, 2] + source_rates[:, 1], source_rates[:, 0]))
    return top_leaving + service_rates[0] + service_rates[1] + sources_top


def source_terms(states, source_rates):
    powers = jnp.cumprod(jnp.full((SOURCES,), 2, jnp.int32)) // 2
    on_bits = ((states[:, None] // powers[None, :]) % 2).astype(source_rates.dtype)
    turn_on = source_rates[:, 0][None, :]
    turn_off = source_rates[:, 1][None, :]
    arrive = source_rates[:, 2][None, :]
    feeding = jnp.sum(on_bits * arrive, axis=1)
    incoming = on_bits * turn_on + (1.0 - on_bits) * turn_off
    outgoing = jnp.sum(on_bits * turn_off + (1.0 - on_bits) * turn_on, axis=1)
    return feeding, incoming, outgoing


def product(tile_data, tile_levels, routes, tables, uniform, service_rates, feeding, incoming, outgoing):
    target = jnp.maximum(routes, 0)
    present = routes >= 0
    top_rim = jnp.where(present[:, 0][:, None, None, None, None], tile_data[target[:, 0], :, :, :, TB1 - BATCH:], 0.0)
    above_bottom = jnp.where(present[:, 1][:, None, None, None], tile_data[target[:, 1], :, :, :, 0], 0.0)
    left_last = jnp.where(present[:, 2][:, None, None, None], tile_data[target[:, 2], :, :, TB2 - 1, :], 0.0)
    right_first = jnp.where(present[:, 3][:, None, None, None], tile_data[target[:, 3], :, :, 0, :], 0.0)
    corner_cell = jnp.where(present[:, 4][:, None, None], tile_data[target[:, 4], :, :, TB2 - 1, 0], 0.0)
    extended = jnp.concatenate([top_rim, tile_data], axis=-1)
    change = jnp.zeros_like(tile_data)
    for offset in range(BATCH + 1):
        window = extended[..., BATCH - offset:BATCH - offset + TB1]
        change = change + jnp.einsum("rspuv,pq->rsquv", window, tables[offset], precision=PRECISE)
    row_ext = jnp.concatenate([tile_data, above_bottom[..., None]], axis=-1)
    side_ext = jnp.concatenate([left_last, corner_cell[..., None]], axis=-1)
    joined = jnp.concatenate([side_ext[..., None, :], row_ext], axis=-2)
    service_one = joined[..., :TB2, 1:]
    service_two = jnp.concatenate([tile_data, right_first[..., None, :]], axis=-2)[..., 1:, :]
    feed_two = jnp.concatenate([left_last[..., None, :], tile_data], axis=-2)[..., :TB2, :]
    for source_bit in range(SOURCES):
        stride = 2 ** source_bit
        shaped = tile_data.reshape((tile_data.shape[0], STATES // (2 * stride), 2, stride) + tile_data.shape[2:])
        partner = jnp.flip(shaped, axis=2).reshape(tile_data.shape)
        change = change + incoming[:, source_bit][None, :, None, None, None] * partner
    first_pos = (tile_levels[:, 0][:, None] * TB1 + jnp.arange(TB1, dtype=jnp.int32)[None, :]) > 0
    second_pos = (tile_levels[:, 1][:, None] * TB2 + jnp.arange(TB2, dtype=jnp.int32)[None, :]) > 0
    leaving_rate = (service_rates[0] * first_pos[:, None, None, None, :]
                    + service_rates[1] * second_pos[:, None, None, :, None]
                    + (feeding + outgoing)[None, :, None, None, None])
    change = (change + service_rates[0] * service_one + service_rates[1] * service_two
              + feeding[None, :, None, None, None] * feed_two - leaving_rate * tile_data)
    return tile_data + change / uniform


def reference(state_values, phase_rates, batch_rates, service_rates, source_rates, tile_levels, routes, tile_owner):
    tables, top_leaving = phase_tables(phase_rates, batch_rates)
    uniform = uniform_rate(top_leaving, service_rates, source_rates)
    states = jnp.arange(STATES, dtype=jnp.int32)
    feeding, incoming, outgoing = source_terms(states, source_rates)
    tile_data = state_values[tile_owner]
    for repeat in range(2):
        tile_data = product(tile_data, tile_levels, routes, tables, uniform, service_rates, feeding, incoming, outgoing)
    return jnp.zeros_like(state_values).at[tile_owner].set(tile_data)
```

```python
import functools

import jax
import jax.numpy as jnp
import numpy as np
from jax import lax
from jax.experimental import pallas as pl
from jax.experimental.pallas import tpu as pltpu
from jax.sharding import PartitionSpec as P

SOURCES = 3
MESH = pl.DeviceIdType.MESH


def split(values):
    high = values.astype(jnp.bfloat16)
    low = (values - high.astype(jnp.float32)).astype(jnp.bfloat16)
    return high, low


def kernel(
    sizes,
    coef,
    leave,
    spots,
    x_ref,
    band_ref,
    out_ref,
    far,
    near,
    mixed,
    high,
    low,
    conv,
    band_cat,
    rows_one,
    rows_two,
    rims_one,
    rims_two,
    bots_one,
    bots_two,
    picks,
    far_send,
    far_recv,
    near_send,
    near_recv,
    pick_send,
    pick_recv,
    edge_send,
    edge_recv,
):
    n_level, n_phase, masks, local_bits, cross, fields = sizes
    C, S, Q, U, V = x_ref.shape
    SU = S * U
    CSU = C * SU
    B = rims_one.shape[-2]
    G = rims_one.shape[-1] // SU
    groups = Q // G
    lanes = G * SU
    level, src, phase = (lax.axis_index(n) for n in ("level", "src", "phase"))
    others = [{"level": lax.rem(level + r, n_level)} for r in range(1, n_level)]
    cores = [{"phase": lax.rem(phase + r, n_phase)} for r in range(1, n_phase)]
    fars = [{"src": jnp.bitwise_xor(src, m)} for m in masks]

    barrier = pltpu.get_barrier_semaphore()
    for device in others + cores + fars:
        pl.semaphore_signal(barrier, inc=1, device_id=device, device_id_type=MESH)
    pl.semaphore_wait(barrier, len(others) + len(cores) + len(fars))

    def send(source, target, sems, index, device):
        copy = pltpu.make_async_remote_copy(
            src_ref=source,
            dst_ref=target,
            send_sem=sems[0].at[index],
            recv_sem=sems[1].at[index],
            device_id=device,
            device_id_type=MESH,
        )
        copy.start()
        return copy

    near_sems = (near_send, near_recv)

    def send_near(source, step):
        return [
            send(source, near.at[step, r], near_sems, step * (n_phase - 1) + r, device)
            for r, device in enumerate(cores)
        ]

    near_copies = send_near(x_ref, 0)
    far_copies = [
        send(x_ref, far.at[m], (far_send, far_recv), m, device) for m, device in enumerate(fars)
    ]

    band_high, band_low = split(band_ref[...])
    M = band_ref.shape[0]
    band_cat[0:M, :] = band_high
    band_cat[M:, :] = band_low

    def put(i, g, first, block):
        turned = block.reshape(CSU, V).T
        top, rest = split(turned)
        at = first + i * G + g
        high[at, B:, :] = top
        low[at, B:, :] = rest
        return turned

    own = pl.ds(level * C, C)
    for step in range(2):
        field = x_ref if step == 0 else mixed
        if step == 1:
            near_copies = send_near(mixed, 1)
        rows, rims, bots = ((rows_one, rims_one, bots_one), (rows_two, rims_two, bots_two))[step]

        def fill_rows(c, carry):
            for s in range(S):
                rows[level * C + c, 0, s] = field[c, s, :, U - 1, :]
                rows[level * C + c, 1, s] = field[c, s, :, 0, :]
                if step == 1:
                    total = jnp.zeros((Q, V), jnp.float32)
                    for k in range(len(cross)):
                        total = total + coef[s * fields + 2 + SOURCES + len(cross) + k + 2] * (
                            far[k, c, s, :, U - 1, :]
                        )
                    rows[level * C + c, 2, s] = total
            return carry

        lax.fori_loop(0, C, fill_rows, 0)

        def turn_own(i, carry):
            turned = [put(i, g, 0, field[:, :, i * G + g]) for g in range(G)]
            for c in range(C):
                part = slice(c * SU, (c + 1) * SU)
                rims[level * C + c, i] = jnp.concatenate(
                    [t[V - B :, part] for t in turned], axis=1
                )
                bots[level * C + c, pl.ds(i, 1), :] = jnp.concatenate(
                    [t[0:1, part] for t in turned], axis=1
                )
            return carry

        lax.fori_loop(0, groups, turn_own, 0)

        edge_copies = []
        for r, device in enumerate(others):
            for a, ref in enumerate(
                (rims.at[own], bots.at[own], rows.at[own])
            ):
                index = (step * (n_level - 1) + r) * 3 + a
                edge_copies.append(send(ref, ref, (edge_send, edge_recv), index, device))

        for r, copy in enumerate(near_copies):
            copy.wait_recv()

            def turn_near(i, carry):
                for g in range(G):
                    put(i, g, (r + 1) * Q, near[step, r, :, :, i * G + g])
                return carry

            lax.fori_loop(0, groups, turn_near, 0)

        for copy in edge_copies:
            copy.wait_recv()

        def spread(i, first, values):
            for g in range(G):
                whole = jnp.concatenate([v[:, g * SU : (g + 1) * SU] for v in values], axis=1)
                top, rest = split(whole)
                high[first + i * G + g, 0:B, :] = top
                low[first + i * G + g, 0:B, :] = rest

        def pick(i, carry):
            values = []
            for c in range(C):
                want = spots[c * 8]
                found = rims[jnp.maximum(want, 0), i]
                value = jnp.where(want >= 0, found, 0.0)
                picks[step, 0, c, i] = value
                values.append(value)
            spread(i, 0, values)
            return carry

        lax.fori_loop(0, groups, pick, 0)
        pick_copies = [
            send(
                picks.at[step, 0],
                picks.at[step, r + 1],
                (pick_send, pick_recv),
                step * (n_phase - 1) + r,
                device,
            )
            for r, device in enumerate(cores)
        ]
        for r, copy in enumerate(pick_copies):
            copy.wait_recv()

            def take(i, carry):
                spread(i, (r + 1) * Q, [picks[step, r + 1, c, i] for c in range(C)])
                return carry

            lax.fori_loop(0, groups, take, 0)

        K = band_ref.shape[1]

        def multiply(v, carry):
            window = pl.ds(pl.multiple_of(v * B, B), 2 * B)
            top = high[:, window, :].reshape(K, CSU)
            rest = low[:, window, :].reshape(K, CSU)
            both = jnp.dot(band_cat[...], top, preferred_element_type=jnp.float32)
            third = jnp.dot(band_cat[0:M, :], rest, preferred_element_type=jnp.float32)
            total = both[0:M] + (both[M:] + third)
            conv[:, pl.ds(pl.multiple_of(v * B, B), B), :] = total.reshape(Q, B, CSU)
            return carry

        lax.fori_loop(0, V // B, multiply, 0)

        def rim_above(i, carry):
            lane = lax.broadcasted_iota(jnp.int32, (8, lanes), 1)
            values = []
            for c in range(C):
                up, corner = spots[c * 8 + 1], spots[c * 8 + 4]
                up_row = jnp.where(up >= 0, bots[jnp.maximum(up, 0), pl.ds(i, 1), :], 0.0)
                corner_row = jnp.where(
                    corner >= 0, bots[jnp.maximum(corner, 0), pl.ds(i, 1), :], 0.0
                )
                up_row = pltpu.roll(jnp.broadcast_to(up_row, (8, lanes)), 1, 1)
                corner_row = pltpu.roll(
                    jnp.broadcast_to(corner_row, (8, lanes)), lanes - (U - 1), 1
                )
                values.append(jnp.where(lane % U == 0, corner_row, up_row))
            for g in range(G):
                whole = jnp.concatenate([v[:, g * SU : (g + 1) * SU] for v in values], axis=1)
                q = i * G + g
                conv[q, V - 1 : V, :] = conv[q, V - 1 : V, :] + coef[0] * whole[0:1]
            return carry

        lax.fori_loop(0, groups, rim_above, 0)

        if step == 0:
            for copy in far_copies:
                copy.wait_recv()

        def combine(q, carry):
            back = conv[q].T
            line = lax.broadcasted_iota(jnp.int32, (U, V), 0)
            lane = lax.broadcasted_iota(jnp.int32, (U, V), 1)
            at = pl.ds(q, 1)

            def side(spot, kind, s):
                found = rows[jnp.maximum(spot, 0), kind, s, at, :]
                return jnp.broadcast_to(jnp.where(spot >= 0, found, 0.0), (U, V))

            for c in range(C):
                base = c * 8
                left, right = spots[base + 2], spots[base + 3]
                gone = (
                    leave[q]
                    + jnp.where(spots[base + 5] * V + lane > 0, coef[0], 0.0)
                    + jnp.where(spots[base + 6] * U + line > 0, coef[1], 0.0)
                )
                blocks = [field[c, s, q] for s in range(S)]
                for s in range(S):
                    here = blocks[s]
                    o = s * fields + 2
                    block = c * S + s
                    value = here + back[block * U : (block + 1) * U]
                    before = jnp.where(line == 0, side(left, 0, s), pltpu.roll(here, 1, 0))
                    after = jnp.where(line == U - 1, side(right, 1, s), pltpu.roll(here, U - 1, 0))
                    moved = jnp.where(lane == V - 1, 0.0, pltpu.roll(before, V - 1, 1))
                    value = value + coef[0] * moved + coef[1] * after + coef[o] * before
                    value = value - (gone + coef[o + 1]) * here
                    for k in range(local_bits):
                        value = value + coef[o + 2 + k] * blocks[s ^ (1 << k)]
                    o = o + 2 + SOURCES
                    n = len(cross)
                    if step == 0:
                        for k in range(n):
                            value = value + coef[o + k] * far[k, c, s, q]
                        mixed[c, s, q] = value
                    else:
                        shifted = jnp.zeros((U, V), jnp.float32)
                        for k in range(n):
                            shifted = shifted + coef[o + n + k] * far[k, c, s, q]
                            value = value + coef[o + 2 * n + k] * far[k, c, s, q]
                        if n:
                            shifted = jnp.where(
                                line == 0, side(left, 2, s), pltpu.roll(shifted, 1, 0)
                            )
                            value = value + shifted + coef[o + 3 * n] * x_ref[c, s, q]
                        for k in range(n, len(masks)):
                            value = value + coef[o + 3 * n + 1 + k - n] * far[k, c, s, q]
                        out_ref[c, s, q] = jnp.where(spots[base + 7] > 0, value, 0.0)
            return carry

        lax.fori_loop(0, Q, combine, 0)
        for copy in near_copies + edge_copies + pick_copies:
            copy.wait_send()
    for copy in far_copies:
        copy.wait_send()


def body(
    n_level,
    n_src,
    n_phase,
    state_values,
    phase_rates,
    batch_rates,
    service_rates,
    source_rates,
    tile_levels,
    routes,
    tile_owner,
):
    C, S, Q, U, V = state_values.shape
    phases = phase_rates.shape[0]
    batch = batch_rates.shape[0]
    local_bits = S.bit_length() - 1
    cross = list(range(local_bits, SOURCES))
    masks = [1 << (k - local_bits) for k in cross]
    pairs = [(a, b) for i, a in enumerate(cross) for b in cross[i + 1 :]]
    masks = masks + [(1 << (a - local_bits)) | (1 << (b - local_bits)) for a, b in pairs]

    moving = phase_rates * (1.0 - jnp.eye(phases, dtype=jnp.float32))
    leaving = jnp.sum(moving, axis=1) + jnp.sum(batch_rates, axis=(0, 2))
    turn_on, turn_off, arrive = source_rates[:, 0], source_rates[:, 1], source_rates[:, 2]
    uniform = (
        jnp.max(leaving)
        + service_rates[0]
        + service_rates[1]
        + jnp.sum(jnp.maximum(arrive + turn_off, turn_on))
    )
    part = lax.axis_index("phase") * Q
    tables = jnp.concatenate([moving[None], batch_rates], axis=0) / uniform
    tables = jnp.roll(lax.dynamic_slice_in_dim(tables, part, Q, 2), -part, axis=1)
    steps = np.arange(batch)[:, None] - np.arange(2 * batch)[None, :] + batch
    hot = (np.arange(batch + 1)[:, None, None] == steps[None]).astype(np.float32)
    band = jnp.einsum("bpq,bvw->qvpw", tables, hot, precision=lax.Precision.HIGHEST)
    band = band.reshape(Q * batch, phases * 2 * batch)
    leave = lax.dynamic_slice_in_dim(leaving, part, Q, 0) / uniform

    states = lax.axis_index("src") * S + jnp.arange(S, dtype=jnp.int32)
    bits = ((states[:, None] >> np.arange(SOURCES, dtype=np.int32)[None, :]) & 1) == 1
    feed = jnp.sum(jnp.where(bits, arrive[None], 0.0), axis=1) / uniform
    inflow = jnp.where(bits, turn_on[None], turn_off[None]) / uniform
    outs = jnp.where(bits, turn_off[None], turn_on[None]) / uniform
    out = jnp.sum(outs, axis=1)
    more_feed = jnp.where(bits, -arrive[None], arrive[None]) / uniform
    more_out = inflow - outs
    columns = [feed, feed + out] + [inflow[:, k] for k in range(SOURCES)]
    columns += [2.0 * inflow[:, k] for k in cross]
    columns += [inflow[:, k] * more_feed[:, k] for k in cross]
    columns += [-inflow[:, k] * (more_feed[:, k] + more_out[:, k]) for k in cross]
    columns += [sum((inflow[:, k] * outs[:, k] for k in cross), jnp.zeros((S,), jnp.float32))]
    columns += [2.0 * inflow[:, a] * inflow[:, b] for a, b in pairs]
    fields = len(columns)
    coef = jnp.concatenate([service_rates / uniform, jnp.stack(columns, axis=1).reshape(-1)])

    holders = lax.axis_index("level") * C + jnp.arange(C, dtype=jnp.int32)
    owned = (tile_owner[None, :] == holders[:, None]).astype(jnp.int32)
    filled = jnp.sum(owned, axis=1)
    slots = jnp.sum(
        jnp.where(
            routes[:, :, None] == jnp.arange(tile_owner.shape[0], dtype=jnp.int32),
            tile_owner[None, None, :] + 1,
            0,
        ),
        axis=2,
    )
    known = jnp.concatenate([slots, tile_levels], axis=1)
    mine = jnp.sum(owned[:, :, None] * known[None], axis=1)
    spots = jnp.concatenate([mine[:, :5] - 1, mine[:, 5:], filled[:, None]], axis=1).reshape(-1)

    group = min(Q, max(1, 128 // (S * U)))
    slot_count = n_level * C
    f32, bf16 = jnp.float32, jnp.bfloat16
    sems = pltpu.SemaphoreType.DMA
    sizes = (n_level, n_phase, masks, local_bits, cross, fields)
    vmem = pl.BlockSpec(memory_space=pltpu.VMEM)
    smem = pl.BlockSpec(memory_space=pltpu.SMEM)
    near_count = max(1, n_phase - 1)
    edge_count = max(1, 6 * (n_level - 1))
    return pl.pallas_call(
        functools.partial(kernel, sizes),
        out_shape=jax.ShapeDtypeStruct(state_values.shape, f32),
        in_specs=[smem, smem, smem, vmem, vmem],
        out_specs=vmem,
        scratch_shapes=[
            pltpu.VMEM((max(1, len(masks)),) + state_values.shape, f32),
            pltpu.VMEM((2, near_count) + state_values.shape, f32),
            pltpu.VMEM(state_values.shape, f32),
            pltpu.VMEM((phases, batch + V, C * S * U), bf16),
            pltpu.VMEM((phases, batch + V, C * S * U), bf16),
            pltpu.VMEM((Q, V, C * S * U), f32),
            pltpu.VMEM((2 * Q * batch, phases * 2 * batch), bf16),
            pltpu.VMEM((slot_count, 2, S, Q, V), f32),
            pltpu.VMEM((slot_count, 3, S, Q, V), f32),
            pltpu.VMEM((slot_count, Q // group, batch, group * S * U), f32),
            pltpu.VMEM((slot_count, Q // group, batch, group * S * U), f32),
            pltpu.VMEM((slot_count, Q // group, group * S * U), f32),
            pltpu.VMEM((slot_count, Q // group, group * S * U), f32),
            pltpu.VMEM((2, n_phase, C, Q // group, batch, group * S * U), f32),
            sems((max(1, len(masks)),)),
            sems((max(1, len(masks)),)),
            sems((2 * near_count,)),
            sems((2 * near_count,)),
            sems((2 * near_count,)),
            sems((2 * near_count,)),
            sems((edge_count,)),
            sems((edge_count,)),
        ],
        compiler_params=pltpu.CompilerParams(
            collective_id=0, has_side_effects=True, vmem_limit_bytes=52 * 1024 * 1024
        ),
    )(coef, leave, spots, state_values, band)


def solution(mesh):
    placed = (
        P(("groups", "level"), "src", "phase", None, None),
        P("groups", None),
        P("groups", None, None),
        P("groups"),
        P("groups", None),
        P("groups", None),
        P("groups", None),
        P("groups"),
    )
    axes = mesh.shape
    return jax.shard_map(
        functools.partial(body, axes["level"], axes["src"], axes["phase"]),
        mesh=mesh,
        in_specs=placed,
        out_specs=P(("groups", "level"), "src", "phase", None, None),
        check_vma=False,
    )
```

```python
import functools

import jax
import jax.numpy as jnp
from jax import lax
from jax.experimental import pallas as pl
from jax.experimental.pallas import tpu as pltpu
from jax.sharding import PartitionSpec as P

SOURCES = 3
MESH = pl.DeviceIdType.MESH


def split(values):
    high = values.astype(jnp.bfloat16)
    low = (values - high.astype(jnp.float32)).astype(jnp.bfloat16)
    return high, low


def kernel(
    sizes,
    service,
    sources,
    levels,
    routes,
    owner,
    x_ref,
    phase_rates,
    batch_rates,
    out_ref,
    far,
    far_edge,
    far_left,
    near,
    mixed,
    high,
    low,
    conv,
    base,
    band,
    band_cat,
    leave,
    edge_one,
    edge_two,
    rim_one,
    rim_two,
    rim_mixed,
    picks,
    left_own,
    far_send,
    far_recv,
    far_edge_send,
    far_edge_recv,
    far_left_send,
    far_left_recv,
    near_send,
    near_recv,
    pick_send,
    pick_recv,
    edge_send,
    edge_recv,
):
    n_level, n_phase, masks, local_bits, cross = sizes
    singles = len(cross)
    C, S, Q, U, V = x_ref.shape
    SU = S * U
    CSU = C * SU
    B = rim_one.shape[-2]
    G = rim_one.shape[-1] // SU
    groups = Q // G
    lanes = G * SU
    phases = n_phase * Q
    wide = 2 * B
    low_at = groups * B
    up_at = low_at + C * S * Q
    bot_at = up_at + C * S * Q
    bot_rows = (edge_one.shape[1] - bot_at) // C
    level, src, phase = (lax.axis_index(n) for n in ("level", "src", "phase"))
    cores = [{"phase": lax.rem(phase + r, n_phase)} for r in range(1, n_phase)]
    fars = [{"src": jnp.bitwise_xor(src, m)} for m in masks]
    sides = ((1, level < n_level - 1, level > 0), (-1, level > 0, level < n_level - 1))

    barrier = pltpu.get_barrier_semaphore()
    for device in cores + fars:
        pl.semaphore_signal(barrier, inc=1, device_id=device, device_id_type=MESH)
    for toward, ahead, behind in sides:

        @pl.when(ahead)
        def _():
            pl.semaphore_signal(
                barrier, inc=1, device_id={"level": level + toward}, device_id_type=MESH
            )

    beside = (level > 0).astype(jnp.int32) + (level < n_level - 1).astype(jnp.int32)
    pl.semaphore_wait(barrier, len(cores) + len(fars) + beside)

    def make(source, target, sems, index, device):
        return pltpu.make_async_remote_copy(
            src_ref=source,
            dst_ref=target,
            send_sem=sems[0].at[index],
            recv_sem=sems[1].at[index],
            device_id=device,
            device_id_type=MESH,
        )

    def send(*parts):
        copy = make(*parts)
        copy.start()
        return copy

    def hop(step, edge, way, h, act):
        toward, ahead, _ = sides[way]
        block = level - toward * h
        index = (step * 2 + way) * (n_level - 1) + h
        held = jnp.logical_and(block >= 0, block < n_level)

        @pl.when(jnp.logical_and(held, ahead))
        def _():
            part = edge.at[block]
            device = {"level": level + toward}
            act(make(part, part, (edge_send, edge_recv), index, device))

    def start_hop(step, edge, h):
        for way in range(2):
            hop(step, edge, way, h, lambda copy: copy.start())

    def end_hop(step, edge, h):
        for way in range(2):
            toward = sides[way][0]
            block = level - toward * (h + 1)
            index = (step * 2 + way) * (n_level - 1) + h

            @pl.when(jnp.logical_and(block >= 0, block < n_level))
            def _():
                part = edge.at[block]
                device = {"level": level - toward}
                make(part, part, (edge_send, edge_recv), index, device).wait_recv()

            if h < n_level - 2:
                hop(step, edge, way, h + 1, lambda copy: copy.start())

    def end_sends(step, edge):
        for h in range(n_level - 1):
            for way in range(2):
                hop(step, edge, way, h, lambda copy: copy.wait_send())

    near_sems = (near_send, near_recv)
    x_near = [
        send(x_ref, near.at[0, r], near_sems, r, device) for r, device in enumerate(cores)
    ]

    tile_count = owner.shape[0]
    spots = []
    count = jnp.int32(0)
    for c in range(C):
        tile, filled = jnp.int32(0), jnp.int32(0)
        for t in range(tile_count):
            here = owner[t] == level * C + c
            tile = jnp.where(here, t, tile)
            filled = jnp.where(here, 1, filled)
        places = []
        for n in range(5):
            route = routes[tile, n]
            slot = owner[jnp.maximum(route, 0)]
            at = lax.div(slot, jnp.int32(C))
            places.append((route >= 0, at, slot - at * C))
        spots.append((places, levels[tile, 0], levels[tile, 1], filled))
        count = count + filled
    last = jnp.maximum(count - 1, 0)

    def turn(field, i, g):
        return field[:, :, i * G + g].reshape(CSU, V).T

    def put(first, i, g, turned):
        top, rest = split(turned)
        high[first + i * G + g, B:, :] = top
        low[first + i * G + g, B:, :] = rest

    def keep_rims(rim, i, turned):
        for c in range(C):
            part = slice(c * SU, (c + 1) * SU)
            rim[c, i] = jnp.concatenate([t[V - B :, part] for t in turned], axis=1)

    def keep_bots(edge, i, turned):
        for c in range(C):
            part = slice(c * SU, (c + 1) * SU)
            edge[level, pl.ds(bot_at + c * bot_rows + i, 1), :] = jnp.concatenate(
                [t[0:1, part] for t in turned], axis=1
            )

    def keep_rows(edge, rim, field):
        for c in range(C):
            for s in range(S):
                at = (c * S + s) * Q
                edge[level, low_at + at : low_at + at + Q, :] = field[c, s, :, U - 1, :]
                edge[level, up_at + at : up_at + at + Q, :] = field[c, s, :, 0, :]
        edge[level, 0:low_at, :] = rim[last].reshape(low_at, lanes)
        if bot_rows > groups:
            for c in range(C):
                at = bot_at + c * bot_rows
                edge[level, at + groups : at + bot_rows, :] = jnp.zeros(
                    (bot_rows - groups, lanes), jnp.float32
                )

    def turn_own(i, carry):
        turned = [turn(x_ref, i, g) for g in range(G)]
        for g in range(G):
            put(0, i, g, turned[g])
        keep_rims(rim_one, i, turned)
        keep_bots(edge_one, i, turned)
        return carry

    lax.fori_loop(0, groups, turn_own, 0)
    keep_rows(edge_one, rim_one, x_ref)
    start_hop(0, edge_one, 0)
    edge_copies = [
        send(edge_one.at[level], far_edge.at[m], (far_edge_send, far_edge_recv), m, device)
        for m, device in enumerate(fars[:singles])
    ]
    far_copies = [
        [
            send(x_ref.at[:, s], far.at[m, :, s], (far_send, far_recv), m * S + s, device)
            for m, device in enumerate(fars)
        ]
        for s in range(S)
    ]

    across = lax.broadcasted_iota(jnp.int32, (phases, phases), 0) == lax.broadcasted_iota(
        jnp.int32, (phases, phases), 1
    )
    moving = jnp.where(across, 0.0, phase_rates[...])
    sums = moving
    for b in range(B):
        sums = sums + batch_rates[b]
    leaving = jnp.sum(sums, axis=1, keepdims=True)
    uniform = jnp.max(leaving) + service[0] + service[1]
    for k in range(SOURCES):
        uniform = uniform + jnp.maximum(sources[k, 2] + sources[k, 1], sources[k, 0])
    inverse = jnp.max(1.0 / jnp.full((8, 128), uniform, jnp.float32))
    leave[...] = jnp.broadcast_to(leaving * inverse, leave.shape)
    serve_one, serve_two = service[0] * inverse, service[1] * inverse
    turn_on = [sources[k, 0] * inverse for k in range(SOURCES)]
    turn_off = [sources[k, 1] * inverse for k in range(SOURCES)]
    arrive = [sources[k, 2] * inverse for k in range(SOURCES)]
    bit = {k: ((src >> (k - local_bits)) & 1) == 1 for k in cross}
    inflow = {k: jnp.where(bit[k], turn_on[k], turn_off[k]) for k in cross}
    outflow = {k: jnp.where(bit[k], turn_off[k], turn_on[k]) for k in cross}
    more_feed = {k: jnp.where(bit[k], -arrive[k], arrive[k]) for k in cross}
    feed, total_out = [], []
    for s in range(S):
        f = o = jnp.float32(0.0)
        for k in range(SOURCES):
            if k in cross:
                f = f + jnp.where(bit[k], arrive[k], 0.0)
                o = o + outflow[k]
            elif s >> k & 1:
                f, o = f + arrive[k], o + turn_off[k]
            else:
                o = o + turn_on[k]
        feed.append(f)
        total_out.append(o)
    twice = [2.0 * inflow[k] for k in cross]
    shift_in = [inflow[k] * more_feed[k] for k in cross]
    stay_in = [-inflow[k] * (more_feed[k] + inflow[k] - outflow[k]) for k in cross]
    back_in = jnp.float32(0.0)
    for k in cross:
        back_in = back_in + inflow[k] * outflow[k]
    pair_in = [
        2.0 * inflow[a] * inflow[b] for i, a in enumerate(cross) for b in cross[i + 1 :]
    ]

    base[...] = jnp.zeros(base.shape, jnp.float32)
    for r in range(n_phase):
        rank = lax.rem(phase + r, n_phase)
        at = pl.ds(pl.multiple_of(rank * Q, Q), Q)
        for w in range(B):
            base[pl.ds(r * Q * wide + w, Q, stride=wide), 0:phases] = (
                batch_rates[B - 1 - w, at, :] * inverse
            )
        row = lax.broadcasted_iota(jnp.int32, (Q, phases), 0) + rank * Q
        column = lax.broadcasted_iota(jnp.int32, (Q, phases), 1)
        base[pl.ds(r * Q * wide + B, Q, stride=wide), 0:phases] = (
            jnp.where(row == column, 0.0, phase_rates[at, :]) * inverse
        )
    out_rows = base[...].T
    base_two = jnp.zeros((Q, phases * wide), jnp.float32)
    for r in range(n_phase):
        base_two = jnp.where(phase == r, out_rows[r * Q : (r + 1) * Q], base_two)
    for v in range(B):
        band[:, v, :] = pltpu.roll(base_two, v, 1) if v else base_two
    M = Q * B
    band_high, band_low = split(band[...].reshape(M, phases * wide))
    band_cat[0:M, :] = band_high
    band_cat[M:, :] = band_low

    def multiply(v, carry):
        window = pl.ds(pl.multiple_of(v * B, B), wide)
        top = high[:, window, :].reshape(phases * wide, CSU)
        rest = low[:, window, :].reshape(phases * wide, CSU)
        both = jnp.dot(band_cat[...], top, preferred_element_type=jnp.float32)
        third = jnp.dot(band_cat[0:M, :], rest, preferred_element_type=jnp.float32)
        total = both[0:M] + (both[M:] + third)
        conv[:, pl.ds(pl.multiple_of(v * B, B), B), :] = total.reshape(Q, B, CSU)
        return carry

    def turn_near(step):
        for r in range(n_phase - 1):

            def one(i, carry):
                for g in range(G):
                    put((r + 1) * Q, i, g, turn(near.at[step, r], i, g))
                return carry

            lax.fori_loop(0, groups, one, 0)

    def spread(i, first, values):
        for g in range(G):
            whole = jnp.concatenate([v[:, g * SU : (g + 1) * SU] for v in values], axis=1)
            top, rest = split(whole)
            high[first + i * G + g, 0:B, :] = top
            low[first + i * G + g, 0:B, :] = rest

    def take_rims(step, edge, rim):
        def pick(i, carry):
            values = []
            for c in range(C):
                there, at, _ = spots[c][0][0]
                if c == 0:
                    found = edge[at, pl.ds(pl.multiple_of(i * B, B), B), :]
                else:
                    found = rim[c - 1, i]
                value = jnp.where(there, found, 0.0)
                picks[step, 0, c, i] = value
                values.append(value)
            spread(i, 0, values)
            return carry

        lax.fori_loop(0, groups, pick, 0)
        copies = [
            send(
                picks.at[step, 0],
                picks.at[step, r + 1],
                (pick_send, pick_recv),
                step * (n_phase - 1) + r,
                device,
            )
            for r, device in enumerate(cores)
        ]
        for r, copy in enumerate(copies):
            copy.wait_recv()

            def take(i, carry):
                spread(i, (r + 1) * Q, [picks[step, r + 1, c, i] for c in range(C)])
                return carry

            lax.fori_loop(0, groups, take, 0)
        multiply(0, 0)
        return copies

    def add_above(edge):
        def one(i, carry):
            lane = lax.broadcasted_iota(jnp.int32, (8, lanes), 1)
            values = []
            for c in range(C):
                rolled = []
                for n, amount in ((1, 1), (4, lanes - (U - 1))):
                    there, at, slot = spots[c][0][n]
                    found = edge[at, pl.ds(bot_at + slot * bot_rows + i, 1), :]
                    found = jnp.broadcast_to(jnp.where(there, found, 0.0), (8, lanes))
                    rolled.append(pltpu.roll(found, amount, 1))
                values.append(jnp.where(lane % U == 0, rolled[1], rolled[0]))
            for g in range(G):
                whole = jnp.concatenate([v[:, g * SU : (g + 1) * SU] for v in values], axis=1)
                q = i * G + g
                conv[q, V - 1 : V, :] = conv[q, V - 1 : V, :] + serve_one * whole[0:1]
            return carry

        lax.fori_loop(0, groups, one, 0)

    def beside_row(edge, place, first, s, q):
        there, at, slot = place
        found = edge[at, pl.ds(first + (slot * S + s) * Q + q, 1), :]
        return jnp.where(there, found, 0.0)

    def combine(step, edge, field):
        def one(q, carry):
            back = conv[q].T
            line = lax.broadcasted_iota(jnp.int32, (U, V), 0)
            lane = lax.broadcasted_iota(jnp.int32, (U, V), 1)
            gone_here = leave[pl.ds(phase * Q + q, 1), :]

            for c in range(C):
                places, level_one, level_two, filled = spots[c]
                gone = (
                    gone_here
                    + jnp.where(level_one * V + lane > 0, serve_one, 0.0)
                    + jnp.where(level_two * U + line > 0, serve_two, 0.0)
                )
                blocks = [field[c, s, q] for s in range(S)]
                for s in range(S):
                    here = blocks[s]
                    block = c * S + s
                    value = here + back[block * U : (block + 1) * U]
                    left = jnp.broadcast_to(beside_row(edge, places[2], low_at, s, q), (U, V))
                    right = jnp.broadcast_to(beside_row(edge, places[3], up_at, s, q), (U, V))
                    before = jnp.where(line == 0, left, pltpu.roll(here, 1, 0))
                    after = jnp.where(line == U - 1, right, pltpu.roll(here, U - 1, 0))
                    moved = jnp.where(lane == V - 1, 0.0, pltpu.roll(before, V - 1, 1))
                    value = value + serve_one * moved + serve_two * after + feed[s] * before
                    value = value - (gone + (feed[s] + total_out[s])) * here
                    for k in range(local_bits):
                        rate = turn_on[k] if s >> k & 1 else turn_off[k]
                        value = value + rate * blocks[s ^ (1 << k)]
                    if step == 0:
                        mixed[c, s, q] = value
                    else:
                        if singles:
                            shifted = jnp.zeros((U, V), jnp.float32)
                            first = jnp.zeros((1, V), jnp.float32)
                            for k in range(singles):
                                other = far[k, c, s, q]
                                shifted = shifted + shift_in[k] * other
                                first = first + shift_in[k] * (
                                    far_left[k, c, pl.ds(s * Q + q, 1), :]
                                )
                                value = value + stay_in[k] * other
                            shifted = jnp.where(
                                line == 0,
                                jnp.broadcast_to(first, (U, V)),
                                pltpu.roll(shifted, 1, 0),
                            )
                            value = value + shifted + back_in * x_ref[c, s, q]
                        for k in range(singles, len(masks)):
                            value = value + pair_in[k - singles] * far[k, c, s, q]
                        out_ref[c, s, q] = jnp.where(filled > 0, value, 0.0)
            return carry

        lax.fori_loop(0, Q, one, 0)

    for copy in x_near:
        copy.wait_recv()
    turn_near(0)
    if n_level > 1:
        end_hop(0, edge_one, 0)
    lax.fori_loop(1, V // B, multiply, 0)
    for h in range(1, n_level - 1):
        end_hop(0, edge_one, h)
    pick_copies = take_rims(0, edge_one, rim_one)
    add_above(edge_one)

    def keep_left(q, carry):
        for c in range(C):
            for s in range(S):
                left_own[c, pl.ds(s * Q + q, 1), :] = beside_row(
                    edge_one, spots[c][0][2], low_at, s, q
                )
        return carry

    lax.fori_loop(0, Q, keep_left, 0)
    left_copies = [
        send(left_own, far_left.at[m], (far_left_send, far_left_recv), m, device)
        for m, device in enumerate(fars[:singles])
    ]
    combine(0, edge_one, x_ref)

    def turn_edges(i, carry):
        turned = [turn(mixed, i, g) for g in range(G)]
        keep_rims(rim_mixed, i, turned)
        keep_bots(edge_two, i, turned)
        return carry

    lax.fori_loop(0, groups, turn_edges, 0)
    keep_rows(edge_two, rim_mixed, mixed)
    for k, copy in enumerate(edge_copies):
        copy.wait_recv()
        edge_two[level] = edge_two[level] + twice[k] * far_edge[k]
    start_hop(1, edge_two, 0)
    mixed_near = []
    for s in range(S):
        for m, copy in enumerate(far_copies[s]):
            copy.wait_recv()
        for c in range(C):

            def add(q, carry):
                value = mixed[c, s, q]
                for k in range(singles):
                    value = value + twice[k] * far[k, c, s, q]
                mixed[c, s, q] = value
                return carry

            lax.fori_loop(0, Q, add, 0)
        for r, device in enumerate(cores):
            index = (n_phase - 1) * (1 + s) + r
            mixed_near.append(
                send(mixed.at[:, s], near.at[1, r, :, s], near_sems, index, device)
            )
        if s == 0 and n_level > 1:
            end_hop(1, edge_two, 0)

    def turn_mixed(i, carry):
        turned = [turn(mixed, i, g) for g in range(G)]
        for g in range(G):
            put(0, i, g, turned[g])
        keep_rims(rim_two, i, turned)
        return carry

    lax.fori_loop(0, groups, turn_mixed, 0)
    if n_level > 2:
        end_hop(1, edge_two, 1)
    for copy in mixed_near:
        copy.wait_recv()
    turn_near(1)
    lax.fori_loop(1, V // B, multiply, 0)
    for h in range(2, n_level - 1):
        end_hop(1, edge_two, h)
    pick_copies += take_rims(1, edge_two, rim_two)
    add_above(edge_two)
    for copy in left_copies:
        copy.wait_recv()
    combine(1, edge_two, mixed)

    for copy in x_near + mixed_near + pick_copies + left_copies + edge_copies:
        copy.wait_send()
    for copies in far_copies:
        for copy in copies:
            copy.wait_send()
    end_sends(0, edge_one)
    end_sends(1, edge_two)


def body(
    n_level,
    n_phase,
    state_values,
    phase_rates,
    batch_rates,
    service_rates,
    source_rates,
    tile_levels,
    routes,
    tile_owner,
):
    C, S, Q, U, V = state_values.shape
    phases = phase_rates.shape[0]
    batch = batch_rates.shape[0]
    local_bits = S.bit_length() - 1
    cross = list(range(local_bits, SOURCES))
    masks = [1 << (k - local_bits) for k in cross]
    masks += [masks[i] | masks[j] for i in range(len(cross)) for j in range(i + 1, len(cross))]
    group = min(Q, max(1, 128 // (S * U)))
    lanes = group * S * U
    groups = Q // group
    edge_rows = groups * batch + 2 * C * S * Q + C * (-(-groups // 8) * 8)
    f32, bf16 = jnp.float32, jnp.bfloat16
    vmem = pl.BlockSpec(memory_space=pltpu.VMEM)
    smem = pl.BlockSpec(memory_space=pltpu.SMEM)
    singles, fars, cores = max(1, len(cross)), max(1, len(masks)), max(1, n_phase - 1)
    counts = [fars * S, singles, singles, cores * (1 + S), 2 * cores, max(1, 4 * (n_level - 1))]
    shapes = [
        ((fars,) + state_values.shape, f32),
        ((singles, edge_rows, lanes), f32),
        ((singles, C, S * Q, V), f32),
        ((2, cores) + state_values.shape, f32),
        (state_values.shape, f32),
        ((phases, batch + V, C * S * U), bf16),
        ((phases, batch + V, C * S * U), bf16),
        ((Q, V, C * S * U), f32),
        ((phases * 2 * batch, 128), f32),
        ((Q, batch, phases * 2 * batch), f32),
        ((2 * Q * batch, phases * 2 * batch), bf16),
        ((phases, V), f32),
        ((n_level, edge_rows, lanes), f32),
        ((n_level, edge_rows, lanes), f32),
        ((C, groups, batch, lanes), f32),
        ((C, groups, batch, lanes), f32),
        ((C, groups, batch, lanes), f32),
        ((2, n_phase, C, groups, batch, lanes), f32),
        ((C, S * Q, V), f32),
    ]
    return pl.pallas_call(
        functools.partial(kernel, (n_level, n_phase, masks, local_bits, cross)),
        out_shape=jax.ShapeDtypeStruct(state_values.shape, f32),
        in_specs=[smem] * 5 + [vmem] * 3,
        out_specs=vmem,
        scratch_shapes=[pltpu.VMEM(*shape) for shape in shapes]
        + [pltpu.SemaphoreType.DMA((n,)) for n in counts for _ in range(2)],
        compiler_params=pltpu.CompilerParams(
            collective_id=0, has_side_effects=True, vmem_limit_bytes=52 * 1024 * 1024
        ),
    )(
        service_rates,
        source_rates,
        tile_levels,
        routes,
        tile_owner,
        state_values,
        phase_rates,
        batch_rates,
    )


def solution(mesh):
    placed = (
        P(("groups", "level"), "src", "phase", None, None),
        P("groups", None),
        P("groups", None, None),
        P("groups"),
        P("groups", None),
        P("groups", None),
        P("groups", None),
        P("groups"),
    )
    axes = mesh.shape
    return jax.shard_map(
        functools.partial(body, axes["level"], axes["phase"]),
        mesh=mesh,
        in_specs=placed,
        out_specs=P(("groups", "level"), "src", "phase", None, None),
        check_vma=False,
    )
```

```python
import functools

import jax
import jax.numpy as jnp
from jax import lax
from jax.experimental import pallas as pl
from jax.experimental.pallas import tpu as pltpu
from jax.sharding import PartitionSpec as P

SOURCES = 3
MESH = pl.DeviceIdType.MESH


def split(values):
    high = values.astype(jnp.bfloat16)
    low = (values - high.astype(jnp.float32)).astype(jnp.bfloat16)
    return high, low


def kernel(
    sizes,
    *refs,
):
    operands, out_ref, held, fetch, rest = refs[:8], refs[8], refs[9:17], refs[17], refs[18:]
    fetches = [
        pltpu.make_async_copy(operand, ref, fetch.at[n])
        for n, (operand, ref) in enumerate(zip(operands, held))
    ]
    for copy in fetches:
        copy.start()
    steps(sizes, fetches, operands[5], *held, out_ref, *rest)


def steps(
    sizes,
    fetches,
    x_hbm,
    service,
    sources,
    levels,
    routes,
    owner,
    x_ref,
    phase_rates,
    batch_rates,
    out_ref,
    far,
    far_edge,
    far_left,
    near,
    mixed,
    high,
    low,
    conv,
    base,
    band,
    band_cat,
    leave,
    edge_one,
    edge_two,
    rim_one,
    rim_two,
    rim_mixed,
    picks,
    left_own,
    far_send,
    far_recv,
    far_edge_send,
    far_edge_recv,
    far_left_send,
    far_left_recv,
    near_send,
    near_recv,
    pick_send,
    pick_recv,
    edge_send,
    edge_recv,
):
    n_level, n_phase, masks, local_bits, cross = sizes
    singles = len(cross)
    C, S, Q, U, V = x_ref.shape
    SU = S * U
    CSU = C * SU
    B = rim_one.shape[-2]
    G = rim_one.shape[-1] // SU
    groups = Q // G
    lanes = G * SU
    phases = n_phase * Q
    wide = 2 * B
    low_at = 0
    up_at = C * S * Q
    rim_at = 2 * C * S * Q
    bot_at = rim_at + groups * B
    bot_rows = (edge_one.shape[1] - bot_at) // C
    parts = (pl.ds(0, rim_at), pl.ds(rim_at, edge_one.shape[1] - rim_at))
    level, src, phase = (lax.axis_index(n) for n in ("level", "src", "phase"))
    cores = [{"phase": lax.rem(phase + r, n_phase)} for r in range(1, n_phase)]
    fars = [{"src": jnp.bitwise_xor(src, m)} for m in masks]
    sides = ((1, level < n_level - 1, level > 0), (-1, level > 0, level < n_level - 1))

    barrier = pltpu.get_barrier_semaphore()
    for device in cores + fars:
        pl.semaphore_signal(barrier, inc=1, device_id=device, device_id_type=MESH)
    for toward, ahead, behind in sides:

        @pl.when(ahead)
        def _():
            pl.semaphore_signal(
                barrier, inc=1, device_id={"level": level + toward}, device_id_type=MESH
            )

    beside = (level > 0).astype(jnp.int32) + (level < n_level - 1).astype(jnp.int32)
    pl.semaphore_wait(barrier, len(cores) + len(fars) + beside)

    def make(source, target, sems, index, device):
        return pltpu.make_async_remote_copy(
            src_ref=source,
            dst_ref=target,
            send_sem=sems[0].at[index],
            recv_sem=sems[1].at[index],
            device_id=device,
            device_id_type=MESH,
        )

    def send(*parts):
        copy = make(*parts)
        copy.start()
        return copy

    def edge_copy(step, edge, part, way, h, block, toward):
        index = ((step * 2 + part) * 2 + way) * (n_level - 1) + h
        piece = edge.at[block, parts[part]]
        return make(piece, piece, (edge_send, edge_recv), index, {"level": level + toward})

    def hop(step, edge, part, way, h, act):
        toward, ahead, _ = sides[way]
        block = level - toward * h
        held = jnp.logical_and(block >= 0, block < n_level)

        @pl.when(jnp.logical_and(held, ahead))
        def _():
            act(edge_copy(step, edge, part, way, h, block, toward))

    def start_hop(step, edge, part):
        for way in range(2):
            hop(step, edge, part, way, 0, lambda copy: copy.start())

    def end_hop(step, edge, part, h):
        for way in range(2):
            toward = sides[way][0]
            block = level - toward * (h + 1)

            @pl.when(jnp.logical_and(block >= 0, block < n_level))
            def _():
                edge_copy(step, edge, part, way, h, block, -toward).wait_recv()

            if h < n_level - 2:
                hop(step, edge, part, way, h + 1, lambda copy: copy.start())

    def end_hops(step, edge, first, end):
        for h in range(first, min(end, n_level - 1)):
            for part in range(2):
                end_hop(step, edge, part, h)

    def end_sends(step, edge):
        for part in range(2):
            for h in range(n_level - 1):
                for way in range(2):
                    hop(step, edge, part, way, h, lambda copy: copy.wait_send())

    near_sems = (near_send, near_recv)
    x_near = [
        send(x_hbm, near.at[0, r], near_sems, r, device) for r, device in enumerate(cores)
    ]
    for copy in fetches:
        copy.wait()

    tile_count = owner.shape[0]
    spots = []
    count = jnp.int32(0)
    for c in range(C):
        tile, filled = jnp.int32(0), jnp.int32(0)
        for t in range(tile_count):
            here = owner[t] == level * C + c
            tile = jnp.where(here, t, tile)
            filled = jnp.where(here, 1, filled)
        places = []
        for n in range(5):
            route = routes[tile, n]
            slot = owner[jnp.maximum(route, 0)]
            at = lax.div(slot, jnp.int32(C))
            places.append((route >= 0, at, slot - at * C))
        spots.append((places, levels[tile, 0], levels[tile, 1], filled))
        count = count + filled
    last = jnp.maximum(count - 1, 0)

    def turn(field, i, g):
        return field[:, :, i * G + g].reshape(CSU, V).T

    def put(first, i, g, turned):
        top, rest = split(turned)
        high[first + i * G + g, B:, :] = top
        low[first + i * G + g, B:, :] = rest

    def keep_rims(rim, i, turned):
        for c in range(C):
            part = slice(c * SU, (c + 1) * SU)
            rim[c, i] = jnp.concatenate([t[V - B :, part] for t in turned], axis=1)

    def keep_bots(edge, i, turned):
        for c in range(C):
            part = slice(c * SU, (c + 1) * SU)
            edge[level, pl.ds(bot_at + c * bot_rows + i, 1), :] = jnp.concatenate(
                [t[0:1, part] for t in turned], axis=1
            )

    def keep_rows(edge, field):
        for c in range(C):
            for s in range(S):
                at = (c * S + s) * Q
                edge[level, low_at + at : low_at + at + Q, :] = field[c, s, :, U - 1, :]
                edge[level, up_at + at : up_at + at + Q, :] = field[c, s, :, 0, :]

    def keep_last(edge, rim):
        edge[level, rim_at:bot_at, :] = rim[last].reshape(bot_at - rim_at, lanes)
        if bot_rows > groups:
            for c in range(C):
                at = bot_at + c * bot_rows
                edge[level, at + groups : at + bot_rows, :] = jnp.zeros(
                    (bot_rows - groups, lanes), jnp.float32
                )

    def turn_own(i, carry):
        turned = [turn(x_ref, i, g) for g in range(G)]
        for g in range(G):
            put(0, i, g, turned[g])
        keep_rims(rim_one, i, turned)
        keep_bots(edge_one, i, turned)
        return carry

    keep_rows(edge_one, x_ref)
    start_hop(0, edge_one, 0)
    lax.fori_loop(0, groups, turn_own, 0)
    keep_last(edge_one, rim_one)
    start_hop(0, edge_one, 1)
    edge_copies = [
        send(edge_one.at[level], far_edge.at[m], (far_edge_send, far_edge_recv), m, device)
        for m, device in enumerate(fars[:singles])
    ]
    far_copies = [
        [
            send(x_hbm.at[:, s], far.at[m, :, s], (far_send, far_recv), m * S + s, device)
            for m, device in enumerate(fars)
        ]
        for s in range(S)
    ]

    across = lax.broadcasted_iota(jnp.int32, (phases, phases), 0) == lax.broadcasted_iota(
        jnp.int32, (phases, phases), 1
    )
    moving = jnp.where(across, 0.0, phase_rates[...])
    sums = moving
    for b in range(B):
        sums = sums + batch_rates[b]
    leaving = jnp.sum(sums, axis=1, keepdims=True)
    uniform = jnp.max(leaving) + service[0] + service[1]
    for k in range(SOURCES):
        uniform = uniform + jnp.maximum(sources[k, 2] + sources[k, 1], sources[k, 0])
    inverse = jnp.max(1.0 / jnp.full((8, 128), uniform, jnp.float32))
    leave[...] = jnp.broadcast_to(leaving * inverse, leave.shape)
    serve_one, serve_two = service[0] * inverse, service[1] * inverse
    turn_on = [sources[k, 0] * inverse for k in range(SOURCES)]
    turn_off = [sources[k, 1] * inverse for k in range(SOURCES)]
    arrive = [sources[k, 2] * inverse for k in range(SOURCES)]
    bit = {k: ((src >> (k - local_bits)) & 1) == 1 for k in cross}
    inflow = {k: jnp.where(bit[k], turn_on[k], turn_off[k]) for k in cross}
    outflow = {k: jnp.where(bit[k], turn_off[k], turn_on[k]) for k in cross}
    more_feed = {k: jnp.where(bit[k], -arrive[k], arrive[k]) for k in cross}
    feed, total_out = [], []
    for s in range(S):
        f = o = jnp.float32(0.0)
        for k in range(SOURCES):
            if k in cross:
                f = f + jnp.where(bit[k], arrive[k], 0.0)
                o = o + outflow[k]
            elif s >> k & 1:
                f, o = f + arrive[k], o + turn_off[k]
            else:
                o = o + turn_on[k]
        feed.append(f)
        total_out.append(o)
    twice = [2.0 * inflow[k] for k in cross]
    shift_in = [inflow[k] * more_feed[k] for k in cross]
    stay_in = [-inflow[k] * (more_feed[k] + inflow[k] - outflow[k]) for k in cross]
    back_in = jnp.float32(0.0)
    for k in cross:
        back_in = back_in + inflow[k] * outflow[k]
    pair_in = [
        2.0 * inflow[a] * inflow[b] for i, a in enumerate(cross) for b in cross[i + 1 :]
    ]

    base[...] = jnp.zeros(base.shape, jnp.float32)
    for r in range(n_phase):
        rank = lax.rem(phase + r, n_phase)
        at = pl.ds(pl.multiple_of(rank * Q, Q), Q)
        for w in range(B):
            base[pl.ds(r * Q * wide + w, Q, stride=wide), 0:phases] = (
                batch_rates[B - 1 - w, at, :] * inverse
            )
        row = lax.broadcasted_iota(jnp.int32, (Q, phases), 0) + rank * Q
        column = lax.broadcasted_iota(jnp.int32, (Q, phases), 1)
        base[pl.ds(r * Q * wide + B, Q, stride=wide), 0:phases] = (
            jnp.where(row == column, 0.0, phase_rates[at, :]) * inverse
        )
    out_rows = base[...].T
    base_two = jnp.zeros((Q, phases * wide), jnp.float32)
    for r in range(n_phase):
        base_two = jnp.where(phase == r, out_rows[r * Q : (r + 1) * Q], base_two)
    for v in range(B):
        band[:, v, :] = pltpu.roll(base_two, v, 1) if v else base_two
    M = Q * B
    band_high, band_low = split(band[...].reshape(M, phases * wide))
    band_cat[0:M, :] = band_high
    band_cat[M:, :] = band_low

    def multiply(v, carry):
        window = pl.ds(pl.multiple_of(v * B, B), wide)
        top = high[:, window, :].reshape(phases * wide, CSU)
        rest = low[:, window, :].reshape(phases * wide, CSU)
        both = jnp.dot(band_cat[...], top, preferred_element_type=jnp.float32)
        third = jnp.dot(band_cat[0:M, :], rest, preferred_element_type=jnp.float32)
        total = both[0:M] + (both[M:] + third)
        conv[:, pl.ds(pl.multiple_of(v * B, B), B), :] = total.reshape(Q, B, CSU)
        return carry

    def turn_near(step):
        for r in range(n_phase - 1):

            def one(i, carry):
                for g in range(G):
                    put((r + 1) * Q, i, g, turn(near.at[step, r], i, g))
                return carry

            lax.fori_loop(0, groups, one, 0)

    def spread(i, first, values):
        for g in range(G):
            whole = jnp.concatenate([v[:, g * SU : (g + 1) * SU] for v in values], axis=1)
            top, rest = split(whole)
            high[first + i * G + g, 0:B, :] = top
            low[first + i * G + g, 0:B, :] = rest

    def take_rims(step, edge, rim):
        def pick(i, carry):
            values = []
            for c in range(C):
                there, at, _ = spots[c][0][0]
                if c == 0:
                    found = edge[at, pl.ds(pl.multiple_of(rim_at + i * B, 8), B), :]
                else:
                    found = rim[c - 1, i]
                value = jnp.where(there, found, 0.0)
                picks[step, 0, c, i] = value
                values.append(value)
            spread(i, 0, values)
            return carry

        lax.fori_loop(0, groups, pick, 0)
        copies = [
            send(
                picks.at[step, 0],
                picks.at[step, r + 1],
                (pick_send, pick_recv),
                step * (n_phase - 1) + r,
                device,
            )
            for r, device in enumerate(cores)
        ]
        for r, copy in enumerate(copies):
            copy.wait_recv()

            def take(i, carry):
                spread(i, (r + 1) * Q, [picks[step, r + 1, c, i] for c in range(C)])
                return carry

            lax.fori_loop(0, groups, take, 0)
        multiply(0, 0)
        return copies

    def add_above(edge):
        def one(i, carry):
            lane = lax.broadcasted_iota(jnp.int32, (8, lanes), 1)
            values = []
            for c in range(C):
                rolled = []
                for n, amount in ((1, 1), (4, lanes - (U - 1))):
                    there, at, slot = spots[c][0][n]
                    found = edge[at, pl.ds(bot_at + slot * bot_rows + i, 1), :]
                    found = jnp.broadcast_to(jnp.where(there, found, 0.0), (8, lanes))
                    rolled.append(pltpu.roll(found, amount, 1))
                values.append(jnp.where(lane % U == 0, rolled[1], rolled[0]))
            for g in range(G):
                whole = jnp.concatenate([v[:, g * SU : (g + 1) * SU] for v in values], axis=1)
                q = i * G + g
                conv[q, V - 1 : V, :] = conv[q, V - 1 : V, :] + serve_one * whole[0:1]
            return carry

        lax.fori_loop(0, groups, one, 0)

    def beside(edge, place, first, s):
        there, at, slot = place
        return jnp.where(there, edge[at, pl.ds(first + (slot * S + s) * Q, Q), :], 0.0)

    def combine(step, field, result):
        def one(q, carry):
            line = lax.broadcasted_iota(jnp.int32, (U, V), 0)
            lane = lax.broadcasted_iota(jnp.int32, (U, V), 1)
            gone_here = leave[pl.ds(phase * Q + q, 1), :]

            for c in range(C):
                _, level_one, level_two, _ = spots[c]
                gone = (
                    gone_here
                    + jnp.where(level_one * V + lane > 0, serve_one, 0.0)
                    + jnp.where(level_two * U + line > 0, serve_two, 0.0)
                )
                blocks = [field[c, s, q] for s in range(S)]
                for s in range(S):
                    here = blocks[s]
                    before = jnp.where(line == 0, 0.0, pltpu.roll(here, 1, 0))
                    after = jnp.where(line == U - 1, 0.0, pltpu.roll(here, U - 1, 0))
                    moved = jnp.where(lane == V - 1, 0.0, pltpu.roll(before, V - 1, 1))
                    value = here - (gone + (feed[s] + total_out[s])) * here
                    value = value + serve_one * moved + serve_two * after + feed[s] * before
                    for k in range(local_bits):
                        rate = turn_on[k] if s >> k & 1 else turn_off[k]
                        value = value + rate * blocks[s ^ (1 << k)]
                    if step == 1:
                        if singles:
                            shifted = jnp.zeros((U, V), jnp.float32)
                            for k in range(singles):
                                other = far[k, c, s, q]
                                shifted = shifted + shift_in[k] * other
                                value = value + stay_in[k] * other
                            shifted = jnp.where(line == 0, 0.0, pltpu.roll(shifted, 1, 0))
                            value = value + shifted + back_in * x_ref[c, s, q]
                        for k in range(singles, len(masks)):
                            value = value + pair_in[k - singles] * far[k, c, s, q]
                    result[c, s, q] = value
            return carry

        lax.fori_loop(0, Q, one, 0)

    def add_rows(step, edge, result):
        lane = lax.broadcasted_iota(jnp.int32, (Q, V), 1)
        for c in range(C):
            places = spots[c][0]
            for s in range(S):
                left = beside(edge, places[2], low_at, s)
                right = beside(edge, places[3], up_at, s)
                moved = jnp.where(lane == V - 1, 0.0, pltpu.roll(left, V - 1, 1))
                added = feed[s] * left + serve_one * moved
                if step == 1:
                    for k in range(singles):
                        added = added + shift_in[k] * far_left[k, c, s * Q : (s + 1) * Q, :]
                result[c, s, :, 0, :] = result[c, s, :, 0, :] + added
                result[c, s, :, U - 1, :] = result[c, s, :, U - 1, :] + serve_two * right

    def finish(step, result):
        def one(q, carry):
            back = conv[q].T.reshape(C, S, U, V)
            for c in range(C):
                value = result[c, :, q] + back[c]
                if step == 1:
                    value = jnp.where(spots[c][3] > 0, value, 0.0)
                result[c, :, q] = value
            return carry

        lax.fori_loop(0, Q, one, 0)

    for copy in x_near:
        copy.wait_recv()
    turn_near(0)
    end_hops(0, edge_one, 0, 1)
    combine(0, x_ref, mixed)
    end_hops(0, edge_one, 1, 2)
    lax.fori_loop(1, V // B, multiply, 0)
    end_hops(0, edge_one, 2, n_level)
    pick_copies = take_rims(0, edge_one, rim_one)
    add_above(edge_one)
    finish(0, mixed)
    add_rows(0, edge_one, mixed)

    def add_far_edges(part):
        for k in range(singles):
            edge_two[level, parts[part]] = (
                edge_two[level, parts[part]] + twice[k] * far_edge[k, parts[part]]
            )
        start_hop(1, edge_two, part)

    keep_rows(edge_two, mixed)
    for copy in edge_copies:
        copy.wait_recv()
    add_far_edges(0)

    def turn_edges(i, carry):
        turned = [turn(mixed, i, g) for g in range(G)]
        keep_rims(rim_mixed, i, turned)
        keep_bots(edge_two, i, turned)
        return carry

    lax.fori_loop(0, groups, turn_edges, 0)
    keep_last(edge_two, rim_mixed)
    add_far_edges(1)

    for c in range(C):
        for s in range(S):
            left_own[c, s * Q : (s + 1) * Q, :] = beside(edge_one, spots[c][0][2], low_at, s)
    left_copies = [
        send(left_own, far_left.at[m], (far_left_send, far_left_recv), m, device)
        for m, device in enumerate(fars[:singles])
    ]

    mixed_near = []
    for s in range(S):
        for copy in far_copies[s]:
            copy.wait_recv()

        def add(q, carry):
            for c in range(C):
                value = mixed[c, s, q]
                for k in range(singles):
                    value = value + twice[k] * far[k, c, s, q]
                mixed[c, s, q] = value
            return carry

        lax.fori_loop(0, Q, add, 0)
        for r, device in enumerate(cores):
            index = (n_phase - 1) * (1 + s) + r
            mixed_near.append(
                send(mixed.at[:, s], near.at[1, r, :, s], near_sems, index, device)
            )

    def turn_mixed(i, carry):
        turned = [turn(mixed, i, g) for g in range(G)]
        for g in range(G):
            put(0, i, g, turned[g])
        keep_rims(rim_two, i, turned)
        return carry

    end_hops(1, edge_two, 0, 1)
    lax.fori_loop(0, groups, turn_mixed, 0)
    for copy in mixed_near:
        copy.wait_recv()
    turn_near(1)
    end_hops(1, edge_two, 1, 2)
    combine(1, mixed, out_ref)
    lax.fori_loop(1, V // B, multiply, 0)
    end_hops(1, edge_two, 2, n_level)
    pick_copies += take_rims(1, edge_two, rim_two)
    add_above(edge_two)
    for copy in left_copies:
        copy.wait_recv()
    add_rows(1, edge_two, out_ref)
    finish(1, out_ref)

    for copy in x_near + mixed_near + pick_copies + left_copies + edge_copies:
        copy.wait_send()
    for copies in far_copies:
        for copy in copies:
            copy.wait_send()
    end_sends(0, edge_one)
    end_sends(1, edge_two)


def body(
    n_level,
    n_phase,
    state_values,
    phase_rates,
    batch_rates,
    service_rates,
    source_rates,
    tile_levels,
    routes,
    tile_owner,
):
    C, S, Q, U, V = state_values.shape
    phases = phase_rates.shape[0]
    batch = batch_rates.shape[0]
    local_bits = S.bit_length() - 1
    cross = list(range(local_bits, SOURCES))
    masks = [1 << (k - local_bits) for k in cross]
    masks += [masks[i] | masks[j] for i in range(len(cross)) for j in range(i + 1, len(cross))]
    group = min(Q, max(1, 128 // (S * U)))
    lanes = group * S * U
    groups = Q // group
    edge_rows = groups * batch + 2 * C * S * Q + C * (-(-groups // 8) * 8)
    f32, bf16 = jnp.float32, jnp.bfloat16
    vmem = pl.BlockSpec(memory_space=pltpu.VMEM)
    singles, fars, cores = max(1, len(cross)), max(1, len(masks)), max(1, n_phase - 1)
    counts = [fars * S, singles, singles, cores * (1 + S), 2 * cores, max(1, 8 * (n_level - 1))]
    shapes = [
        ((fars,) + state_values.shape, f32),
        ((singles, edge_rows, lanes), f32),
        ((singles, C, S * Q, V), f32),
        ((2, cores) + state_values.shape, f32),
        (state_values.shape, f32),
        ((phases, batch + V, C * S * U), bf16),
        ((phases, batch + V, C * S * U), bf16),
        ((Q, V, C * S * U), f32),
        ((phases * 2 * batch, 128), f32),
        ((Q, batch, phases * 2 * batch), f32),
        ((2 * Q * batch, phases * 2 * batch), bf16),
        ((phases, V), f32),
        ((n_level, edge_rows, lanes), f32),
        ((n_level, edge_rows, lanes), f32),
        ((C, groups, batch, lanes), f32),
        ((C, groups, batch, lanes), f32),
        ((C, groups, batch, lanes), f32),
        ((2, n_phase, C, groups, batch, lanes), f32),
        ((C, S * Q, V), f32),
    ]
    operands = (
        service_rates,
        source_rates,
        tile_levels,
        routes,
        tile_owner,
        state_values,
        phase_rates,
        batch_rates,
    )
    return pl.pallas_call(
        functools.partial(kernel, (n_level, n_phase, masks, local_bits, cross)),
        out_shape=jax.ShapeDtypeStruct(state_values.shape, f32),
        in_specs=[pl.BlockSpec(memory_space=pl.ANY)] * 8,
        out_specs=vmem,
        scratch_shapes=[pltpu.SMEM(a.shape, a.dtype) for a in operands[:5]]
        + [pltpu.VMEM(a.shape, a.dtype) for a in operands[5:]]
        + [pltpu.SemaphoreType.DMA((len(operands),))]
        + [pltpu.VMEM(*shape) for shape in shapes]
        + [pltpu.SemaphoreType.DMA((n,)) for n in counts for _ in range(2)],
        compiler_params=pltpu.CompilerParams(
            collective_id=0, has_side_effects=True, vmem_limit_bytes=52 * 1024 * 1024
        ),
    )(*operands)


def solution(mesh):
    placed = (
        P(("groups", "level"), "src", "phase", None, None),
        P("groups", None),
        P("groups", None, None),
        P("groups"),
        P("groups", None),
        P("groups", None),
        P("groups", None),
        P("groups"),
    )
    axes = mesh.shape
    return jax.shard_map(
        functools.partial(body, axes["level"], axes["phase"]),
        mesh=mesh,
        in_specs=placed,
        out_specs=P(("groups", "level"), "src", "phase", None, None),
        check_vma=False,
    )
```

```python
import functools

import jax
import jax.numpy as jnp
from jax import lax
from jax.experimental import pallas as pl
from jax.experimental.pallas import tpu as pltpu
from jax.sharding import PartitionSpec as P

SOURCES = 3
MESH = pl.DeviceIdType.MESH


def split(values):
    high = values.astype(jnp.bfloat16)
    low = (values - high.astype(jnp.float32)).astype(jnp.bfloat16)
    return high, low


def kernel(
    sizes,
    *refs,
):
    operands, out_ref, held, fetch, rest = refs[:8], refs[8], refs[9:17], refs[17], refs[18:]
    fetches = [
        pltpu.make_async_copy(operand, ref, fetch.at[n])
        for n, (operand, ref) in enumerate(zip(operands, held))
    ]
    for copy in fetches:
        copy.start()
    steps(sizes, fetches, operands[5], *held, out_ref, *rest)


def steps(
    sizes,
    fetches,
    x_hbm,
    service,
    sources,
    levels,
    routes,
    owner,
    x_ref,
    phase_rates,
    batch_rates,
    out_ref,
    far,
    far_edge,
    far_left,
    near,
    mixed,
    high,
    low,
    conv,
    base,
    band,
    band_cat,
    leave,
    edge_one,
    edge_two,
    rim_one,
    rim_two,
    rim_mixed,
    picks,
    left_own,
    far_send,
    far_recv,
    far_edge_send,
    far_edge_recv,
    far_left_send,
    far_left_recv,
    near_send,
    near_recv,
    pick_send,
    pick_recv,
    edge_send,
    edge_recv,
):
    n_level, n_phase, masks, local_bits, cross = sizes
    singles = len(cross)
    C, S, Q, U, V = x_ref.shape
    halves = 2 if S > 1 else 1
    H = S // halves
    HU = H * U
    used = C * HU
    stride = high.shape[-1] // halves
    B = rim_one.shape[-2]
    G = rim_one.shape[-1] // (S * U)
    groups = Q // G
    lanes = G * S * U
    phases = n_phase * Q
    wide = 2 * B
    low_at = 0
    up_at = C * S * Q
    rim_at = 2 * C * S * Q
    bot_at = rim_at + groups * B
    bot_rows = (edge_one.shape[1] - bot_at) // C
    parts = (pl.ds(0, rim_at), pl.ds(rim_at, edge_one.shape[1] - rim_at))
    level, src, phase = (lax.axis_index(n) for n in ("level", "src", "phase"))
    cores = [{"phase": lax.rem(phase + r, n_phase)} for r in range(1, n_phase)]
    fars = [{"src": jnp.bitwise_xor(src, m)} for m in masks]
    sides = ((1, level < n_level - 1, level > 0), (-1, level > 0, level < n_level - 1))

    barrier = pltpu.get_barrier_semaphore()
    for device in cores + fars:
        pl.semaphore_signal(barrier, inc=1, device_id=device, device_id_type=MESH)
    for toward, ahead, behind in sides:

        @pl.when(ahead)
        def _():
            pl.semaphore_signal(
                barrier, inc=1, device_id={"level": level + toward}, device_id_type=MESH
            )

    beside = (level > 0).astype(jnp.int32) + (level < n_level - 1).astype(jnp.int32)
    pl.semaphore_wait(barrier, len(cores) + len(fars) + beside)

    def make(source, target, sems, index, device):
        return pltpu.make_async_remote_copy(
            src_ref=source,
            dst_ref=target,
            send_sem=sems[0].at[index],
            recv_sem=sems[1].at[index],
            device_id=device,
            device_id_type=MESH,
        )

    def send(*parts):
        copy = make(*parts)
        copy.start()
        return copy

    def edge_copy(step, edge, part, way, h, block, toward):
        index = ((step * 2 + part) * 2 + way) * (n_level - 1) + h
        piece = edge.at[block, parts[part]]
        return make(piece, piece, (edge_send, edge_recv), index, {"level": level + toward})

    def hop(step, edge, part, way, h, act):
        toward, ahead, _ = sides[way]
        block = level - toward * h
        held = jnp.logical_and(block >= 0, block < n_level)

        @pl.when(jnp.logical_and(held, ahead))
        def _():
            act(edge_copy(step, edge, part, way, h, block, toward))

    def start_hop(step, edge, part):
        for way in range(2):
            hop(step, edge, part, way, 0, lambda copy: copy.start())

    def end_hop(step, edge, part, h):
        for way in range(2):
            toward = sides[way][0]
            block = level - toward * (h + 1)

            @pl.when(jnp.logical_and(block >= 0, block < n_level))
            def _():
                edge_copy(step, edge, part, way, h, block, -toward).wait_recv()

            if h < n_level - 2:
                hop(step, edge, part, way, h + 1, lambda copy: copy.start())

    def end_hops(step, edge, first, end):
        for h in range(first, min(end, n_level - 1)):
            for part in range(2):
                end_hop(step, edge, part, h)

    def end_sends(step, edge):
        for part in range(2):
            for h in range(n_level - 1):
                for way in range(2):
                    hop(step, edge, part, way, h, lambda copy: copy.wait_send())

    near_sems = (near_send, near_recv)
    x_near = [
        send(x_hbm, near.at[0, r], near_sems, r, device) for r, device in enumerate(cores)
    ]

    def send_far(s):
        return [
            send(x_hbm.at[:, s], far.at[m, :, s], (far_send, far_recv), m * S + s, device)
            for m, device in enumerate(fars)
        ]

    far_copies = [send_far(0)]
    for copy in fetches:
        copy.wait()

    for h in range(halves):
        if used < stride:
            gap = (phases, B + V, stride - used)
            high[:, :, h * stride + used : (h + 1) * stride] = jnp.zeros(gap, jnp.bfloat16)
            low[:, :, h * stride + used : (h + 1) * stride] = jnp.zeros(gap, jnp.bfloat16)

    tile_count = owner.shape[0]
    spots = []
    count = jnp.int32(0)
    for c in range(C):
        tile, filled = jnp.int32(0), jnp.int32(0)
        for t in range(tile_count):
            here = owner[t] == level * C + c
            tile = jnp.where(here, t, tile)
            filled = jnp.where(here, 1, filled)
        places = []
        for n in range(5):
            route = routes[tile, n]
            slot = owner[jnp.maximum(route, 0)]
            at = lax.div(slot, jnp.int32(C))
            places.append((route >= 0, at, slot - at * C))
        spots.append((places, levels[0, tile], levels[1, tile], filled))
        count = count + filled
    last = jnp.maximum(count - 1, 0)

    def turn(field, h, i, g):
        return field[:, h * H : (h + 1) * H, i * G + g].reshape(used, V).T

    def put(first, h, i, g, turned):
        top, rest = split(turned)
        high[first + i * G + g, B:, h * stride : h * stride + used] = top
        low[first + i * G + g, B:, h * stride : h * stride + used] = rest

    def group_lanes(turned, rows, c):
        return jnp.concatenate([t[rows, c * HU : (c + 1) * HU] for t in turned], axis=1)

    def keep_rims(rim, i, turned):
        for c in range(C):
            rim[c, i] = group_lanes(turned, slice(V - B, V), c)

    def keep_bots(edge, i, turned):
        for c in range(C):
            edge[level, pl.ds(bot_at + c * bot_rows + i, 1), :] = group_lanes(
                turned, slice(0, 1), c
            )

    def turn_all(field, i):
        return [turn(field, h, i, g) for h in range(halves) for g in range(G)]

    def keep_rows(edge, field):
        for c in range(C):
            for s in range(S):
                at = (c * S + s) * Q
                edge[level, low_at + at : low_at + at + Q, :] = field[c, s, :, U - 1, :]
                edge[level, up_at + at : up_at + at + Q, :] = field[c, s, :, 0, :]

    def keep_last(edge, rim):
        edge[level, rim_at:bot_at, :] = rim[last].reshape(bot_at - rim_at, lanes)
        if bot_rows > groups:
            for c in range(C):
                at = bot_at + c * bot_rows
                edge[level, at + groups : at + bot_rows, :] = jnp.zeros(
                    (bot_rows - groups, lanes), jnp.float32
                )

    def turn_own(i, carry):
        turned = turn_all(x_ref, i)
        for h in range(halves):
            for g in range(G):
                put(0, h, i, g, turned[h * G + g])
        keep_rims(rim_one, i, turned)
        keep_bots(edge_one, i, turned)
        return carry

    keep_rows(edge_one, x_ref)
    start_hop(0, edge_one, 0)
    lax.fori_loop(0, groups, turn_own, 0)
    keep_last(edge_one, rim_one)
    start_hop(0, edge_one, 1)
    edge_copies = [
        send(edge_one.at[level], far_edge.at[m], (far_edge_send, far_edge_recv), m, device)
        for m, device in enumerate(fars[:singles])
    ]
    far_copies += [send_far(s) for s in range(1, S)]

    across = lax.broadcasted_iota(jnp.int32, (phases, phases), 0) == lax.broadcasted_iota(
        jnp.int32, (phases, phases), 1
    )
    moving = jnp.where(across, 0.0, phase_rates[...])
    sums = moving
    for b in range(B):
        sums = sums + batch_rates[b]
    leaving = jnp.sum(sums, axis=1, keepdims=True)
    uniform = jnp.max(leaving) + service[0] + service[1]
    for k in range(SOURCES):
        uniform = uniform + jnp.maximum(sources[k, 2] + sources[k, 1], sources[k, 0])
    inverse = jnp.max(1.0 / jnp.full((8, 128), uniform, jnp.float32))
    leave[...] = jnp.broadcast_to(leaving * inverse, leave.shape)
    serve_one, serve_two = service[0] * inverse, service[1] * inverse
    turn_on = [sources[k, 0] * inverse for k in range(SOURCES)]
    turn_off = [sources[k, 1] * inverse for k in range(SOURCES)]
    arrive = [sources[k, 2] * inverse for k in range(SOURCES)]
    bit = {k: ((src >> (k - local_bits)) & 1) == 1 for k in cross}
    inflow = {k: jnp.where(bit[k], turn_on[k], turn_off[k]) for k in cross}
    outflow = {k: jnp.where(bit[k], turn_off[k], turn_on[k]) for k in cross}
    more_feed = {k: jnp.where(bit[k], -arrive[k], arrive[k]) for k in cross}
    feed, total_out = [], []
    for s in range(S):
        f = o = jnp.float32(0.0)
        for k in range(SOURCES):
            if k in cross:
                f = f + jnp.where(bit[k], arrive[k], 0.0)
                o = o + outflow[k]
            elif s >> k & 1:
                f, o = f + arrive[k], o + turn_off[k]
            else:
                o = o + turn_on[k]
        feed.append(f)
        total_out.append(o)
    twice = [2.0 * inflow[k] for k in cross]
    shift_in = [inflow[k] * more_feed[k] for k in cross]
    stay_in = [-inflow[k] * (more_feed[k] + inflow[k] - outflow[k]) for k in cross]
    back_in = jnp.float32(0.0)
    for k in cross:
        back_in = back_in + inflow[k] * outflow[k]
    pair_in = [
        2.0 * inflow[a] * inflow[b] for i, a in enumerate(cross) for b in cross[i + 1 :]
    ]

    base[...] = jnp.zeros(base.shape, jnp.float32)
    for r in range(n_phase):
        rank = lax.rem(phase + r, n_phase)
        at = pl.ds(pl.multiple_of(rank * Q, Q), Q)
        for w in range(B):
            base[pl.ds(r * Q * wide + w, Q, stride=wide), 0:phases] = (
                batch_rates[B - 1 - w, at, :] * inverse
            )
        row = lax.broadcasted_iota(jnp.int32, (Q, phases), 0) + rank * Q
        column = lax.broadcasted_iota(jnp.int32, (Q, phases), 1)
        base[pl.ds(r * Q * wide + B, Q, stride=wide), 0:phases] = (
            jnp.where(row == column, 0.0, phase_rates[at, :]) * inverse
        )
    out_rows = base[...].T
    base_two = jnp.zeros((Q, phases * wide), jnp.float32)
    for r in range(n_phase):
        base_two = jnp.where(phase == r, out_rows[r * Q : (r + 1) * Q], base_two)
    for v in range(B):
        band[:, v, :] = pltpu.roll(base_two, v, 1) if v else base_two
    M = Q * B
    band_high, band_low = split(band[...].reshape(M, phases * wide))
    band_cat[0:M, :] = band_high
    band_cat[M:, :] = band_low

    def multiply(v, carry):
        window = pl.ds(pl.multiple_of(v * B, B), wide)
        top = high[:, window, :].reshape(phases * wide, halves * stride)
        rest = low[:, window, :].reshape(phases * wide, halves * stride)
        both = jnp.dot(band_cat[...], top, preferred_element_type=jnp.float32)
        third = jnp.dot(band_cat[0:M, :], rest, preferred_element_type=jnp.float32)
        total = both[0:M] + (both[M:] + third)
        conv[:, pl.ds(pl.multiple_of(v * B, B), B), :] = total.reshape(Q, B, halves * stride)
        return carry

    def turn_near(step, which):
        for r in range(n_phase - 1):

            def one(i, carry):
                for h in which:
                    for g in range(G):
                        put((r + 1) * Q, h, i, g, turn(near.at[step, r], h, i, g))
                return carry

            lax.fori_loop(0, groups, one, 0)

    def by_half(values, h, g):
        at = (h * G + g) * HU
        return jnp.concatenate([v[:, at : at + HU] for v in values], axis=1)

    def spread(i, first, values):
        for h in range(halves):
            for g in range(G):
                top, rest = split(by_half(values, h, g))
                high[first + i * G + g, 0:B, h * stride : h * stride + used] = top
                low[first + i * G + g, 0:B, h * stride : h * stride + used] = rest

    def take_rims(step, edge, rim):
        def pick(i, carry):
            values = []
            for c in range(C):
                there, at, _ = spots[c][0][0]
                if c == 0:
                    found = edge[at, pl.ds(pl.multiple_of(rim_at + i * B, 8), B), :]
                else:
                    found = rim[c - 1, i]
                value = jnp.where(there, found, 0.0)
                picks[step, 0, c, i] = value
                values.append(value)
            spread(i, 0, values)
            return carry

        lax.fori_loop(0, groups, pick, 0)
        return [
            send(
                picks.at[step, 0],
                picks.at[step, r + 1],
                (pick_send, pick_recv),
                step * (n_phase - 1) + r,
                device,
            )
            for r, device in enumerate(cores)
        ]

    def share_rims(step, copies):
        for r, copy in enumerate(copies):
            copy.wait_recv()

            def take(i, carry):
                spread(i, (r + 1) * Q, [picks[step, r + 1, c, i] for c in range(C)])
                return carry

            lax.fori_loop(0, groups, take, 0)

    def add_above(edge):
        def one(i, carry):
            lane = lax.broadcasted_iota(jnp.int32, (8, lanes), 1)
            values = []
            for c in range(C):
                rolled = []
                for n, amount in ((1, 1), (4, lanes - (U - 1))):
                    there, at, slot = spots[c][0][n]
                    found = edge[at, pl.ds(bot_at + slot * bot_rows + i, 1), :]
                    found = jnp.broadcast_to(jnp.where(there, found, 0.0), (8, lanes))
                    rolled.append(pltpu.roll(found, amount, 1))
                values.append(jnp.where(lane % U == 0, rolled[1], rolled[0]))
            for h in range(halves):
                part = slice(h * stride, h * stride + used)
                for g in range(G):
                    whole = by_half(values, h, g)
                    q = i * G + g
                    conv[q, V - 1 : V, part] = conv[q, V - 1 : V, part] + serve_one * whole[0:1]
            return carry

        lax.fori_loop(0, groups, one, 0)

    def beside(edge, place, first, s):
        there, at, slot = place
        return jnp.where(there, edge[at, pl.ds(first + (slot * S + s) * Q, Q), :], 0.0)

    def gone_from(c, q, line, lane):
        _, level_one, level_two, _ = spots[c]
        return (
            leave[pl.ds(phase * Q + q, 1), :]
            + jnp.where(level_one * V + lane > 0, serve_one, 0.0)
            + jnp.where(level_two * U + line > 0, serve_two, 0.0)
        )

    def within(s, here, gone, line, lane):
        before = jnp.where(line == 0, 0.0, pltpu.roll(here, 1, 0))
        after = jnp.where(line == U - 1, 0.0, pltpu.roll(here, U - 1, 0))
        moved = jnp.where(lane == V - 1, 0.0, pltpu.roll(before, V - 1, 1))
        value = here - (gone + (feed[s] + total_out[s])) * here
        return value + serve_one * moved + serve_two * after + feed[s] * before

    def flip_rate(s, k):
        return turn_on[k] if s >> k & 1 else turn_off[k]

    def combine(step, field, result):
        def one(q, carry):
            line = lax.broadcasted_iota(jnp.int32, (U, V), 0)
            lane = lax.broadcasted_iota(jnp.int32, (U, V), 1)
            for c in range(C):
                gone = gone_from(c, q, line, lane)
                blocks = [field[c, s, q] for s in range(S)]
                for s in range(S):
                    value = within(s, blocks[s], gone, line, lane)
                    for k in range(local_bits):
                        value = value + flip_rate(s, k) * blocks[s ^ (1 << k)]
                    if step == 1 and singles:
                        value = value + back_in * x_ref[c, s, q]
                    result[c, s, q] = value
            return carry

        lax.fori_loop(0, Q, one, 0)

    def add_far(s):
        def one(q, carry):
            for c in range(C):
                value = mixed[c, s, q]
                for k in range(singles):
                    value = value + twice[k] * far[k, c, s, q]
                mixed[c, s, q] = value
            return carry

        lax.fori_loop(0, Q, one, 0)

    def combine_far(s):
        def one(q, carry):
            line = lax.broadcasted_iota(jnp.int32, (U, V), 0)
            lane = lax.broadcasted_iota(jnp.int32, (U, V), 1)
            for c in range(C):
                here = shifted = stay = jnp.zeros((U, V), jnp.float32)
                for k in range(singles):
                    other = far[k, c, s, q]
                    here = here + twice[k] * other
                    shifted = shifted + shift_in[k] * other
                    stay = stay + stay_in[k] * other
                for k in range(singles, len(masks)):
                    stay = stay + pair_in[k - singles] * far[k, c, s, q]
                value = within(s, here, gone_from(c, q, line, lane), line, lane) + stay
                value = value + jnp.where(line == 0, 0.0, pltpu.roll(shifted, 1, 0))
                out_ref[c, s, q] = out_ref[c, s, q] + value
                for k in range(local_bits):
                    t = s ^ (1 << k)
                    out_ref[c, t, q] = out_ref[c, t, q] + flip_rate(t, k) * here
            return carry

        lax.fori_loop(0, Q, one, 0)

    def add_rows(step, edge, result):
        lane = lax.broadcasted_iota(jnp.int32, (Q, V), 1)
        for c in range(C):
            places = spots[c][0]
            for s in range(S):
                left = beside(edge, places[2], low_at, s)
                right = beside(edge, places[3], up_at, s)
                moved = jnp.where(lane == V - 1, 0.0, pltpu.roll(left, V - 1, 1))
                added = feed[s] * left + serve_one * moved
                if step == 1:
                    for k in range(singles):
                        added = added + shift_in[k] * far_left[k, c, s * Q : (s + 1) * Q, :]
                result[c, s, :, 0, :] = result[c, s, :, 0, :] + added
                result[c, s, :, U - 1, :] = result[c, s, :, U - 1, :] + serve_two * right

    def finish(step, result):
        def one(q, carry):
            for h in range(halves):
                back = conv[q, :, h * stride : (h + 1) * stride].T[0:used].reshape(C, H, U, V)
                for c in range(C):
                    value = result[c, h * H : (h + 1) * H, q] + back[c]
                    if step == 1:
                        value = jnp.where(spots[c][3] > 0, value, 0.0)
                    result[c, h * H : (h + 1) * H, q] = value
            return carry

        lax.fori_loop(0, Q, one, 0)

    for copy in x_near:
        copy.wait_recv()
    turn_near(0, range(halves))
    end_hops(0, edge_one, 0, 1)
    combine(0, x_ref, mixed)
    end_hops(0, edge_one, 1, 2)
    lax.fori_loop(1, V // B, multiply, 0)
    end_hops(0, edge_one, 2, n_level)
    pick_copies = take_rims(0, edge_one, rim_one)
    add_above(edge_one)
    add_rows(0, edge_one, mixed)
    share_rims(0, pick_copies)
    multiply(0, 0)
    finish(0, mixed)

    def add_far_edges(part):
        for k in range(singles):
            edge_two[level, parts[part]] = (
                edge_two[level, parts[part]] + twice[k] * far_edge[k, parts[part]]
            )
        start_hop(1, edge_two, part)

    keep_rows(edge_two, mixed)
    for copy in edge_copies:
        copy.wait_recv()
    add_far_edges(0)

    def turn_edges(i, carry):
        turned = turn_all(mixed, i)
        keep_rims(rim_mixed, i, turned)
        keep_bots(edge_two, i, turned)
        return carry

    lax.fori_loop(0, groups, turn_edges, 0)
    keep_last(edge_two, rim_mixed)
    add_far_edges(1)

    for c in range(C):
        for s in range(S):
            left_own[c, s * Q : (s + 1) * Q, :] = beside(edge_one, spots[c][0][2], low_at, s)
    left_copies = [
        send(left_own, far_left.at[m], (far_left_send, far_left_recv), m, device)
        for m, device in enumerate(fars[:singles])
    ]

    combine(1, mixed, out_ref)
    end_hops(1, edge_two, 0, 1)

    def turn_mixed(h):
        def one(i, carry):
            for g in range(G):
                turned = turn(mixed, h, i, g)
                put(0, h, i, g, turned)
                for c in range(C):
                    at = (h * G + g) * HU
                    rim_two[c, i, :, at : at + HU] = turned[V - B :, c * HU : (c + 1) * HU]
            return carry

        lax.fori_loop(0, groups, one, 0)

    mixed_near = []
    for s in range(S):
        for copy in far_copies[s]:
            copy.wait_recv()
        add_far(s)
        if s == 0:
            end_hops(1, edge_two, 1, 2)
        fresh = []
        for r, device in enumerate(cores):
            index = (n_phase - 1) * (1 + s) + r
            fresh.append(send(mixed.at[:, s], near.at[1, r, :, s], near_sems, index, device))
        mixed_near += fresh
        if s == S - 1:
            turn_mixed(halves - 1)
            end_hops(1, edge_two, 2, n_level)
            last_picks = take_rims(1, edge_two, rim_two)
            pick_copies += last_picks
        combine_far(s)
        for copy in fresh:
            copy.wait_recv()
        if (s + 1) % H == 0:
            if s < S - 1:
                turn_mixed(s // H)
            turn_near(1, [s // H])
    share_rims(1, last_picks)
    lax.fori_loop(0, V // B, multiply, 0)
    add_above(edge_two)
    for copy in left_copies:
        copy.wait_recv()
    add_rows(1, edge_two, out_ref)
    finish(1, out_ref)

    for copy in x_near + mixed_near + pick_copies + left_copies + edge_copies:
        copy.wait_send()
    for copies in far_copies:
        for copy in copies:
            copy.wait_send()
    end_sends(0, edge_one)
    end_sends(1, edge_two)


def body(
    n_level,
    n_phase,
    state_values,
    phase_rates,
    batch_rates,
    service_rates,
    source_rates,
    tile_levels,
    routes,
    tile_owner,
):
    C, S, Q, U, V = state_values.shape
    phases = phase_rates.shape[0]
    batch = batch_rates.shape[0]
    local_bits = S.bit_length() - 1
    cross = list(range(local_bits, SOURCES))
    masks = [1 << (k - local_bits) for k in cross]
    masks += [masks[i] | masks[j] for i in range(len(cross)) for j in range(i + 1, len(cross))]
    group = min(Q, max(1, 128 // (S * U)))
    lanes = group * S * U
    groups = Q // group
    halves = 2 if S > 1 else 1
    width = halves * (-(-(C * S * U // halves) // 128) * 128)
    edge_rows = groups * batch + 2 * C * S * Q + C * (-(-groups // 8) * 8)
    f32, bf16 = jnp.float32, jnp.bfloat16
    vmem = pl.BlockSpec(memory_space=pltpu.VMEM)
    singles, fars, cores = max(1, len(cross)), max(1, len(masks)), max(1, n_phase - 1)
    counts = [fars * S, singles, singles, cores * (1 + S), 2 * cores, max(1, 8 * (n_level - 1))]
    shapes = [
        ((fars,) + state_values.shape, f32),
        ((singles, edge_rows, lanes), f32),
        ((singles, C, S * Q, V), f32),
        ((2, cores) + state_values.shape, f32),
        (state_values.shape, f32),
        ((phases, batch + V, width), bf16),
        ((phases, batch + V, width), bf16),
        ((Q, V, width), f32),
        ((phases * 2 * batch, 128), f32),
        ((Q, batch, phases * 2 * batch), f32),
        ((2 * Q * batch, phases * 2 * batch), bf16),
        ((phases, V), f32),
        ((n_level, edge_rows, lanes), f32),
        ((n_level, edge_rows, lanes), f32),
        ((C, groups, batch, lanes), f32),
        ((C, groups, batch, lanes), f32),
        ((C, groups, batch, lanes), f32),
        ((2, n_phase, C, groups, batch, lanes), f32),
        ((C, S * Q, V), f32),
    ]
    operands = (
        service_rates,
        source_rates,
        tile_levels.T,
        routes,
        tile_owner,
        state_values,
        phase_rates,
        batch_rates,
    )
    return pl.pallas_call(
        functools.partial(kernel, (n_level, n_phase, masks, local_bits, cross)),
        out_shape=jax.ShapeDtypeStruct(state_values.shape, f32),
        in_specs=[pl.BlockSpec(memory_space=pl.ANY)] * 8,
        out_specs=vmem,
        scratch_shapes=[pltpu.SMEM(a.shape, a.dtype) for a in operands[:5]]
        + [pltpu.VMEM(a.shape, a.dtype) for a in operands[5:]]
        + [pltpu.SemaphoreType.DMA((len(operands),))]
        + [pltpu.VMEM(*shape) for shape in shapes]
        + [pltpu.SemaphoreType.DMA((n,)) for n in counts for _ in range(2)],
        compiler_params=pltpu.CompilerParams(
            collective_id=0, has_side_effects=True, vmem_limit_bytes=60 * 1024 * 1024
        ),
    )(*operands)


def solution(mesh):
    placed = (
        P(("groups", "level"), "src", "phase", None, None),
        P("groups", None),
        P("groups", None, None),
        P("groups"),
        P("groups", None),
        P("groups", None),
        P("groups", None),
        P("groups"),
    )
    axes = mesh.shape
    return jax.shard_map(
        functools.partial(body, axes["level"], axes["phase"]),
        mesh=mesh,
        in_specs=placed,
        out_specs=P(("groups", "level"), "src", "phase", None, None),
        check_vma=False,
    )
```

```python
import functools

import jax
import jax.numpy as jnp
from jax import lax
from jax.experimental import pallas as pl
from jax.experimental.pallas import tpu as pltpu
from jax.sharding import PartitionSpec as P

SOURCES = 3
MESH = pl.DeviceIdType.MESH


def split(values):
    high = values.astype(jnp.bfloat16)
    low = (values - high.astype(jnp.float32)).astype(jnp.bfloat16)
    return high, low


def kernel(
    sizes,
    *refs,
):
    operands, out_ref, held, fetch, rest = refs[:8], refs[8], refs[9:17], refs[17], refs[18:]
    fetches = [
        pltpu.make_async_copy(operand, ref, fetch.at[n])
        for n, (operand, ref) in enumerate(zip(operands, held))
    ]
    for copy in fetches:
        copy.start()
    steps(sizes, fetches, operands[5], *held, out_ref, *rest)


def steps(
    sizes,
    fetches,
    x_hbm,
    service,
    sources,
    levels,
    routes,
    owner,
    x_ref,
    phase_rates,
    batch_rates,
    out_ref,
    far,
    far_edge,
    far_left,
    near,
    mixed,
    high,
    low,
    conv,
    base,
    band,
    band_cat,
    leave,
    edge_one,
    edge_two,
    rim_one,
    rim_two,
    rim_mixed,
    picks,
    left_own,
    far_send,
    far_recv,
    far_edge_send,
    far_edge_recv,
    far_left_send,
    far_left_recv,
    near_send,
    near_recv,
    pick_send,
    pick_recv,
    edge_send,
    edge_recv,
):
    n_level, n_phase, masks, local_bits, cross = sizes
    singles = len(cross)
    C, S, Q, U, V = x_ref.shape
    halves = 2 if S > 1 else 1
    H = S // halves
    HU = H * U
    used = C * HU
    stride = high.shape[-1] // halves
    B = rim_one.shape[-2]
    G = rim_one.shape[-1] // (S * U)
    groups = Q // G
    lanes = G * S * U
    phases = n_phase * Q
    wide = 2 * B
    low_at = 0
    up_at = C * S * Q
    rim_at = 2 * C * S * Q
    bot_at = rim_at + groups * B
    bot_rows = (edge_one.shape[1] - bot_at) // C
    parts = (pl.ds(0, rim_at), pl.ds(rim_at, edge_one.shape[1] - rim_at))
    level, src, phase = (lax.axis_index(n) for n in ("level", "src", "phase"))
    cores = [{"phase": lax.rem(phase + r, n_phase)} for r in range(1, n_phase)]
    fars = [{"src": jnp.bitwise_xor(src, m)} for m in masks]
    sides = ((1, level < n_level - 1, level > 0), (-1, level > 0, level < n_level - 1))

    barrier = pltpu.get_barrier_semaphore()
    for device in cores + fars:
        pl.semaphore_signal(barrier, inc=1, device_id=device, device_id_type=MESH)
    for toward, ahead, behind in sides:

        @pl.when(ahead)
        def _():
            pl.semaphore_signal(
                barrier, inc=1, device_id={"level": level + toward}, device_id_type=MESH
            )

    beside = (level > 0).astype(jnp.int32) + (level < n_level - 1).astype(jnp.int32)
    pl.semaphore_wait(barrier, len(cores) + len(fars) + beside)

    def make(source, target, sems, index, device):
        return pltpu.make_async_remote_copy(
            src_ref=source,
            dst_ref=target,
            send_sem=sems[0].at[index],
            recv_sem=sems[1].at[index],
            device_id=device,
            device_id_type=MESH,
        )

    def send(*parts):
        copy = make(*parts)
        copy.start()
        return copy

    def edge_copy(step, edge, part, way, h, block, toward):
        index = ((step * 2 + part) * 2 + way) * (n_level - 1) + h
        piece = edge.at[block, parts[part]]
        return make(piece, piece, (edge_send, edge_recv), index, {"level": level + toward})

    def hop(step, edge, part, way, h, act):
        toward, ahead, _ = sides[way]
        block = level - toward * h
        held = jnp.logical_and(block >= 0, block < n_level)

        @pl.when(jnp.logical_and(held, ahead))
        def _():
            act(edge_copy(step, edge, part, way, h, block, toward))

    def start_hop(step, edge, part):
        for way in range(2):
            hop(step, edge, part, way, 0, lambda copy: copy.start())

    def end_hop(step, edge, part, h):
        for way in range(2):
            toward = sides[way][0]
            block = level - toward * (h + 1)

            @pl.when(jnp.logical_and(block >= 0, block < n_level))
            def _():
                edge_copy(step, edge, part, way, h, block, -toward).wait_recv()

            if h < n_level - 2:
                hop(step, edge, part, way, h + 1, lambda copy: copy.start())

    def end_hops(step, edge, first, end):
        for h in range(first, min(end, n_level - 1)):
            for part in range(2):
                end_hop(step, edge, part, h)

    def end_sends(step, edge):
        for part in range(2):
            for h in range(n_level - 1):
                for way in range(2):
                    hop(step, edge, part, way, h, lambda copy: copy.wait_send())

    near_sems = (near_send, near_recv)
    x_near = [
        send(x_hbm, near.at[0, r], near_sems, r, device) for r, device in enumerate(cores)
    ]

    def send_far(s):
        return [
            send(x_hbm.at[:, s], far.at[m, :, s], (far_send, far_recv), m * S + s, device)
            for m, device in enumerate(fars)
        ]

    far_copies = [send_far(0)]
    for copy in fetches:
        copy.wait()

    for h in range(halves):
        if used < stride:
            gap = (phases, B + V, stride - used)
            high[:, :, h * stride + used : (h + 1) * stride] = jnp.zeros(gap, jnp.bfloat16)
            low[:, :, h * stride + used : (h + 1) * stride] = jnp.zeros(gap, jnp.bfloat16)

    tile_count = owner.shape[0]
    spots = []
    count = jnp.int32(0)
    for c in range(C):
        tile, filled = jnp.int32(0), jnp.int32(0)
        for t in range(tile_count):
            here = owner[t] == level * C + c
            tile = jnp.where(here, t, tile)
            filled = jnp.where(here, 1, filled)
        places = []
        for n in range(5):
            route = routes[tile, n]
            slot = owner[jnp.maximum(route, 0)]
            at = lax.div(slot, jnp.int32(C))
            places.append((route >= 0, at, slot - at * C))
        spots.append((places, levels[0, tile], levels[1, tile], filled))
        count = count + filled
    last = jnp.maximum(count - 1, 0)

    def turn(field, h, i, g):
        return field[:, h * H : (h + 1) * H, i * G + g].reshape(used, V).T

    def put(first, h, i, g, turned):
        top, rest = split(turned)
        high[first + i * G + g, B:, h * stride : h * stride + used] = top
        low[first + i * G + g, B:, h * stride : h * stride + used] = rest

    def group_lanes(turned, rows, c):
        return jnp.concatenate([t[rows, c * HU : (c + 1) * HU] for t in turned], axis=1)

    def keep_rims(rim, i, turned):
        for c in range(C):
            rim[c, i] = group_lanes(turned, slice(V - B, V), c)

    def keep_bots(edge, i, turned):
        for c in range(C):
            edge[level, pl.ds(bot_at + c * bot_rows + i, 1), :] = group_lanes(
                turned, slice(0, 1), c
            )

    def turn_all(field, i):
        return [turn(field, h, i, g) for h in range(halves) for g in range(G)]

    def keep_rows(edge, field):
        for c in range(C):
            for s in range(S):
                at = (c * S + s) * Q
                edge[level, low_at + at : low_at + at + Q, :] = field[c, s, :, U - 1, :]
                edge[level, up_at + at : up_at + at + Q, :] = field[c, s, :, 0, :]

    def keep_last(edge, rim):
        edge[level, rim_at:bot_at, :] = rim[last].reshape(bot_at - rim_at, lanes)
        if bot_rows > groups:
            for c in range(C):
                at = bot_at + c * bot_rows
                edge[level, at + groups : at + bot_rows, :] = jnp.zeros(
                    (bot_rows - groups, lanes), jnp.float32
                )

    def turn_own(i, carry):
        turned = turn_all(x_ref, i)
        for h in range(halves):
            for g in range(G):
                put(0, h, i, g, turned[h * G + g])
        keep_rims(rim_one, i, turned)
        keep_bots(edge_one, i, turned)
        return carry

    keep_rows(edge_one, x_ref)
    start_hop(0, edge_one, 0)
    lax.fori_loop(0, groups, turn_own, 0)
    keep_last(edge_one, rim_one)
    start_hop(0, edge_one, 1)
    edge_copies = [
        send(edge_one.at[level], far_edge.at[m], (far_edge_send, far_edge_recv), m, device)
        for m, device in enumerate(fars[:singles])
    ]
    far_copies += [send_far(s) for s in range(1, S)]

    across = lax.broadcasted_iota(jnp.int32, (phases, phases), 0) == lax.broadcasted_iota(
        jnp.int32, (phases, phases), 1
    )
    moving = jnp.where(across, 0.0, phase_rates[...])
    sums = moving
    for b in range(B):
        sums = sums + batch_rates[b]
    leaving = jnp.sum(sums, axis=1, keepdims=True)
    uniform = jnp.max(leaving) + service[0] + service[1]
    for k in range(SOURCES):
        uniform = uniform + jnp.maximum(sources[k, 2] + sources[k, 1], sources[k, 0])
    inverse = jnp.max(1.0 / jnp.full((8, 128), uniform, jnp.float32))
    leave[...] = jnp.broadcast_to(leaving * inverse, leave.shape)
    serve_one, serve_two = service[0] * inverse, service[1] * inverse
    turn_on = [sources[k, 0] * inverse for k in range(SOURCES)]
    turn_off = [sources[k, 1] * inverse for k in range(SOURCES)]
    arrive = [sources[k, 2] * inverse for k in range(SOURCES)]
    bit = {k: ((src >> (k - local_bits)) & 1) == 1 for k in cross}
    inflow = {k: jnp.where(bit[k], turn_on[k], turn_off[k]) for k in cross}
    outflow = {k: jnp.where(bit[k], turn_off[k], turn_on[k]) for k in cross}
    more_feed = {k: jnp.where(bit[k], -arrive[k], arrive[k]) for k in cross}
    feed, total_out = [], []
    for s in range(S):
        f = o = jnp.float32(0.0)
        for k in range(SOURCES):
            if k in cross:
                f = f + jnp.where(bit[k], arrive[k], 0.0)
                o = o + outflow[k]
            elif s >> k & 1:
                f, o = f + arrive[k], o + turn_off[k]
            else:
                o = o + turn_on[k]
        feed.append(f)
        total_out.append(o)
    twice = [2.0 * inflow[k] for k in cross]
    shift_in = [inflow[k] * more_feed[k] for k in cross]
    stay_in = [-inflow[k] * (more_feed[k] + inflow[k] - outflow[k]) for k in cross]
    back_in = jnp.float32(0.0)
    for k in cross:
        back_in = back_in + inflow[k] * outflow[k]
    pair_in = [
        2.0 * inflow[a] * inflow[b] for i, a in enumerate(cross) for b in cross[i + 1 :]
    ]

    base[...] = jnp.zeros(base.shape, jnp.float32)
    for r in range(n_phase):
        rank = lax.rem(phase + r, n_phase)
        at = pl.ds(pl.multiple_of(rank * Q, Q), Q)
        for w in range(B):
            base[pl.ds(r * Q * wide + w, Q, stride=wide), 0:phases] = (
                batch_rates[B - 1 - w, at, :] * inverse
            )
        row = lax.broadcasted_iota(jnp.int32, (Q, phases), 0) + rank * Q
        column = lax.broadcasted_iota(jnp.int32, (Q, phases), 1)
        base[pl.ds(r * Q * wide + B, Q, stride=wide), 0:phases] = (
            jnp.where(row == column, 0.0, phase_rates[at, :]) * inverse
        )
    out_rows = base[...].T
    base_two = jnp.zeros((Q, phases * wide), jnp.float32)
    for r in range(n_phase):
        base_two = jnp.where(phase == r, out_rows[r * Q : (r + 1) * Q], base_two)
    for v in range(B):
        band[:, v, :] = pltpu.roll(base_two, v, 1) if v else base_two
    M = Q * B
    band_high, band_low = split(band[...].reshape(M, phases * wide))
    band_cat[0:M, :] = band_high
    band_cat[M:, :] = band_low

    def multiply(v, carry):
        window = pl.ds(pl.multiple_of(v * B, B), wide)
        top = high[:, window, :].reshape(phases * wide, halves * stride)
        rest = low[:, window, :].reshape(phases * wide, halves * stride)
        both = jnp.dot(band_cat[...], top, preferred_element_type=jnp.float32)
        third = jnp.dot(band_cat[0:M, :], rest, preferred_element_type=jnp.float32)
        total = both[0:M] + (both[M:] + third)
        conv[:, pl.ds(pl.multiple_of(v * B, B), B), :] = total.reshape(Q, B, halves * stride)
        return carry

    def turn_near(step, which):
        for r in range(n_phase - 1):

            def one(i, carry):
                for h in which:
                    for g in range(G):
                        put((r + 1) * Q, h, i, g, turn(near.at[step, r], h, i, g))
                return carry

            lax.fori_loop(0, groups, one, 0)

    def by_half(values, h, g):
        at = (h * G + g) * HU
        return jnp.concatenate([v[:, at : at + HU] for v in values], axis=1)

    def spread(i, first, values):
        for h in range(halves):
            for g in range(G):
                top, rest = split(by_half(values, h, g))
                high[first + i * G + g, 0:B, h * stride : h * stride + used] = top
                low[first + i * G + g, 0:B, h * stride : h * stride + used] = rest

    def take_rims(step, edge, rim):
        def pick(i, carry):
            values = []
            for c in range(C):
                there, at, _ = spots[c][0][0]
                if c == 0:
                    found = edge[at, pl.ds(pl.multiple_of(rim_at + i * B, 8), B), :]
                else:
                    found = rim[c - 1, i]
                value = jnp.where(there, found, 0.0)
                picks[step, 0, c, i] = value
                values.append(value)
            spread(i, 0, values)
            return carry

        lax.fori_loop(0, groups, pick, 0)
        return [
            send(
                picks.at[step, 0],
                picks.at[step, r + 1],
                (pick_send, pick_recv),
                step * (n_phase - 1) + r,
                device,
            )
            for r, device in enumerate(cores)
        ]

    def share_rims(step, copies):
        for r, copy in enumerate(copies):
            copy.wait_recv()

            def take(i, carry):
                spread(i, (r + 1) * Q, [picks[step, r + 1, c, i] for c in range(C)])
                return carry

            lax.fori_loop(0, groups, take, 0)

    def add_above(edge):
        def one(i, carry):
            lane = lax.broadcasted_iota(jnp.int32, (8, lanes), 1)
            values = []
            for c in range(C):
                rolled = []
                for n, amount in ((1, 1), (4, lanes - (U - 1))):
                    there, at, slot = spots[c][0][n]
                    found = edge[at, pl.ds(bot_at + slot * bot_rows + i, 1), :]
                    found = jnp.broadcast_to(jnp.where(there, found, 0.0), (8, lanes))
                    rolled.append(pltpu.roll(found, amount, 1))
                values.append(jnp.where(lane % U == 0, rolled[1], rolled[0]))
            for h in range(halves):
                part = slice(h * stride, h * stride + used)
                for g in range(G):
                    whole = by_half(values, h, g)
                    q = i * G + g
                    conv[q, V - 1 : V, part] = conv[q, V - 1 : V, part] + serve_one * whole[0:1]
            return carry

        lax.fori_loop(0, groups, one, 0)

    def beside(edge, place, first, s):
        there, at, slot = place
        return jnp.where(there, edge[at, pl.ds(first + (slot * S + s) * Q, Q), :], 0.0)

    def gone_from(c, q, line, lane):
        _, level_one, level_two, _ = spots[c]
        return (
            leave[pl.ds(phase * Q + q, 1), :]
            + jnp.where(level_one * V + lane > 0, serve_one, 0.0)
            + jnp.where(level_two * U + line > 0, serve_two, 0.0)
        )

    def within(s, here, gone, line, lane):
        before = jnp.where(line == 0, 0.0, pltpu.roll(here, 1, 0))
        after = jnp.where(line == U - 1, 0.0, pltpu.roll(here, U - 1, 0))
        moved = jnp.where(lane == V - 1, 0.0, pltpu.roll(before, V - 1, 1))
        value = here - (gone + (feed[s] + total_out[s])) * here
        return value + serve_one * moved + serve_two * after + feed[s] * before

    def flip_rate(s, k):
        return turn_on[k] if s >> k & 1 else turn_off[k]

    def combine(step, field, result):
        def one(q, carry):
            line = lax.broadcasted_iota(jnp.int32, (U, V), 0)
            lane = lax.broadcasted_iota(jnp.int32, (U, V), 1)
            for c in range(C):
                gone = gone_from(c, q, line, lane)
                blocks = [field[c, s, q] for s in range(S)]
                for s in range(S):
                    value = within(s, blocks[s], gone, line, lane)
                    for k in range(local_bits):
                        value = value + flip_rate(s, k) * blocks[s ^ (1 << k)]
                    if step == 1 and singles:
                        value = value + back_in * x_ref[c, s, q]
                    result[c, s, q] = value
            return carry

        lax.fori_loop(0, Q, one, 0)

    def add_far(s):
        def one(q, carry):
            for c in range(C):
                value = mixed[c, s, q]
                for k in range(singles):
                    value = value + twice[k] * far[k, c, s, q]
                mixed[c, s, q] = value
            return carry

        lax.fori_loop(0, Q, one, 0)

    def combine_far(s):
        def one(q, carry):
            line = lax.broadcasted_iota(jnp.int32, (U, V), 0)
            lane = lax.broadcasted_iota(jnp.int32, (U, V), 1)
            for c in range(C):
                here = shifted = stay = jnp.zeros((U, V), jnp.float32)
                for k in range(singles):
                    other = far[k, c, s, q]
                    here = here + twice[k] * other
                    shifted = shifted + shift_in[k] * other
                    stay = stay + stay_in[k] * other
                for k in range(singles, len(masks)):
                    stay = stay + pair_in[k - singles] * far[k, c, s, q]
                value = within(s, here, gone_from(c, q, line, lane), line, lane) + stay
                value = value + jnp.where(line == 0, 0.0, pltpu.roll(shifted, 1, 0))
                out_ref[c, s, q] = out_ref[c, s, q] + value
                for k in range(local_bits):
                    t = s ^ (1 << k)
                    out_ref[c, t, q] = out_ref[c, t, q] + flip_rate(t, k) * here
            return carry

        lax.fori_loop(0, Q, one, 0)

    def add_rows(step, edge, result):
        lane = lax.broadcasted_iota(jnp.int32, (Q, V), 1)
        for c in range(C):
            places = spots[c][0]
            for s in range(S):
                left = beside(edge, places[2], low_at, s)
                right = beside(edge, places[3], up_at, s)
                moved = jnp.where(lane == V - 1, 0.0, pltpu.roll(left, V - 1, 1))
                added = feed[s] * left + serve_one * moved
                if step == 1:
                    for k in range(singles):
                        added = added + shift_in[k] * far_left[k, c, s * Q : (s + 1) * Q, :]
                result[c, s, :, 0, :] = result[c, s, :, 0, :] + added
                result[c, s, :, U - 1, :] = result[c, s, :, U - 1, :] + serve_two * right

    def finish(step, result):
        def one(q, carry):
            for h in range(halves):
                back = conv[q, :, h * stride : (h + 1) * stride].T[0:used].reshape(C, H, U, V)
                for c in range(C):
                    value = result[c, h * H : (h + 1) * H, q] + back[c]
                    if step == 1:
                        value = jnp.where(spots[c][3] > 0, value, 0.0)
                    result[c, h * H : (h + 1) * H, q] = value
            return carry

        lax.fori_loop(0, Q, one, 0)

    end_hops(0, edge_one, 0, 1)
    for copy in x_near:
        copy.wait_recv()
    turn_near(0, range(halves))
    combine(0, x_ref, mixed)
    end_hops(0, edge_one, 1, 2)
    lax.fori_loop(1, V // B, multiply, 0)
    end_hops(0, edge_one, 2, n_level)
    pick_copies = take_rims(0, edge_one, rim_one)
    add_above(edge_one)
    add_rows(0, edge_one, mixed)
    share_rims(0, pick_copies)
    multiply(0, 0)
    finish(0, mixed)

    def add_far_edges(part):
        for k in range(singles):
            edge_two[level, parts[part]] = (
                edge_two[level, parts[part]] + twice[k] * far_edge[k, parts[part]]
            )
        start_hop(1, edge_two, part)

    keep_rows(edge_two, mixed)
    for copy in edge_copies:
        copy.wait_recv()
    add_far_edges(0)

    def turn_edges(i, carry):
        for c in range(C):
            pieces = [
                mixed[c, h * H : (h + 1) * H, i * G + g].reshape(HU, V)
                for h in range(halves)
                for g in range(G)
            ]
            turned = jnp.concatenate(pieces, axis=0).T
            rim_mixed[c, i] = turned[V - B :]
            edge_two[level, pl.ds(bot_at + c * bot_rows + i, 1), :] = turned[0:1]
        return carry

    lax.fori_loop(0, groups, turn_edges, 0)
    keep_last(edge_two, rim_mixed)
    add_far_edges(1)
    if n_level > 1:
        end_hop(1, edge_two, 0, 0)

    for c in range(C):
        for s in range(S):
            left_own[c, s * Q : (s + 1) * Q, :] = beside(edge_one, spots[c][0][2], low_at, s)
    left_copies = [
        send(left_own, far_left.at[m], (far_left_send, far_left_recv), m, device)
        for m, device in enumerate(fars[:singles])
    ]

    combine(1, mixed, out_ref)
    if n_level > 1:
        end_hop(1, edge_two, 1, 0)

    def turn_mixed(h):
        def one(i, carry):
            for g in range(G):
                turned = turn(mixed, h, i, g)
                put(0, h, i, g, turned)
                for c in range(C):
                    at = (h * G + g) * HU
                    rim_two[c, i, :, at : at + HU] = turned[V - B :, c * HU : (c + 1) * HU]
            return carry

        lax.fori_loop(0, groups, one, 0)

    mixed_near = []
    for s in range(S):
        for copy in far_copies[s]:
            copy.wait_recv()
        add_far(s)
        fresh = []
        for r, device in enumerate(cores):
            index = (n_phase - 1) * (1 + s) + r
            fresh.append(send(mixed.at[:, s], near.at[1, r, :, s], near_sems, index, device))
        mixed_near += fresh
        if s == S - 1:
            turn_mixed(halves - 1)
        combine_far(s)
        for copy in fresh:
            copy.wait_recv()
        if (s + 1) % H == 0:
            if s < S - 1:
                turn_mixed(s // H)
            turn_near(1, [s // H])
        if s == max(0, S // 2 - 1):
            end_hops(1, edge_two, 1, 2)
    lax.fori_loop(1, V // B, multiply, 0)
    end_hops(1, edge_two, 2, n_level)
    last_picks = take_rims(1, edge_two, rim_two)
    pick_copies += last_picks
    add_above(edge_two)
    for copy in left_copies:
        copy.wait_recv()
    add_rows(1, edge_two, out_ref)
    share_rims(1, last_picks)
    multiply(0, 0)
    finish(1, out_ref)

    for copy in x_near + mixed_near + pick_copies + left_copies + edge_copies:
        copy.wait_send()
    for copies in far_copies:
        for copy in copies:
            copy.wait_send()
    end_sends(0, edge_one)
    end_sends(1, edge_two)


def body(
    n_level,
    n_phase,
    state_values,
    phase_rates,
    batch_rates,
    service_rates,
    source_rates,
    tile_levels,
    routes,
    tile_owner,
):
    C, S, Q, U, V = state_values.shape
    phases = phase_rates.shape[0]
    batch = batch_rates.shape[0]
    local_bits = S.bit_length() - 1
    cross = list(range(local_bits, SOURCES))
    masks = [1 << (k - local_bits) for k in cross]
    masks += [masks[i] | masks[j] for i in range(len(cross)) for j in range(i + 1, len(cross))]
    group = min(Q, max(1, 128 // (S * U)))
    lanes = group * S * U
    groups = Q // group
    halves = 2 if S > 1 else 1
    width = halves * (-(-(C * S * U // halves) // 128) * 128)
    edge_rows = groups * batch + 2 * C * S * Q + C * (-(-groups // 8) * 8)
    f32, bf16 = jnp.float32, jnp.bfloat16
    vmem = pl.BlockSpec(memory_space=pltpu.VMEM)
    singles, fars, cores = max(1, len(cross)), max(1, len(masks)), max(1, n_phase - 1)
    counts = [fars * S, singles, singles, cores * (1 + S), 2 * cores, max(1, 8 * (n_level - 1))]
    shapes = [
        ((fars,) + state_values.shape, f32),
        ((singles, edge_rows, lanes), f32),
        ((singles, C, S * Q, V), f32),
        ((2, cores) + state_values.shape, f32),
        (state_values.shape, f32),
        ((phases, batch + V, width), bf16),
        ((phases, batch + V, width), bf16),
        ((Q, V, width), f32),
        ((phases * 2 * batch, 128), f32),
        ((Q, batch, phases * 2 * batch), f32),
        ((2 * Q * batch, phases * 2 * batch), bf16),
        ((phases, V), f32),
        ((n_level, edge_rows, lanes), f32),
        ((n_level, edge_rows, lanes), f32),
        ((C, groups, batch, lanes), f32),
        ((C, groups, batch, lanes), f32),
        ((C, groups, batch, lanes), f32),
        ((2, n_phase, C, groups, batch, lanes), f32),
        ((C, S * Q, V), f32),
    ]
    operands = (
        service_rates,
        source_rates,
        tile_levels.T,
        routes,
        tile_owner,
        state_values,
        phase_rates,
        batch_rates,
    )
    return pl.pallas_call(
        functools.partial(kernel, (n_level, n_phase, masks, local_bits, cross)),
        out_shape=jax.ShapeDtypeStruct(state_values.shape, f32),
        in_specs=[pl.BlockSpec(memory_space=pl.ANY)] * 8,
        out_specs=vmem,
        scratch_shapes=[pltpu.SMEM(a.shape, a.dtype) for a in operands[:5]]
        + [pltpu.VMEM(a.shape, a.dtype) for a in operands[5:]]
        + [pltpu.SemaphoreType.DMA((len(operands),))]
        + [pltpu.VMEM(*shape) for shape in shapes]
        + [pltpu.SemaphoreType.DMA((n,)) for n in counts for _ in range(2)],
        compiler_params=pltpu.CompilerParams(
            collective_id=0, has_side_effects=True, vmem_limit_bytes=60 * 1024 * 1024
        ),
    )(*operands)


def solution(mesh):
    placed = (
        P(("groups", "level"), "src", "phase", None, None),
        P("groups", None),
        P("groups", None, None),
        P("groups"),
        P("groups", None),
        P("groups", None),
        P("groups", None),
        P("groups"),
    )
    axes = mesh.shape
    return jax.shard_map(
        functools.partial(body, axes["level"], axes["phase"]),
        mesh=mesh,
        in_specs=placed,
        out_specs=P(("groups", "level"), "src", "phase", None, None),
        check_vma=False,
    )
```

```python
import functools

import jax
import jax.numpy as jnp
from jax import lax
from jax.experimental import pallas as pl
from jax.experimental.pallas import tpu as pltpu
from jax.sharding import PartitionSpec as P

SOURCES = 3
MESH = pl.DeviceIdType.MESH


def split(values):
    high = values.astype(jnp.bfloat16)
    low = (values - high.astype(jnp.float32)).astype(jnp.bfloat16)
    return high, low


def kernel(
    sizes,
    *refs,
):
    operands, out_ref, held, fetch, rest = refs[:8], refs[8], refs[9:17], refs[17], refs[18:]
    fetches = [
        pltpu.make_async_copy(operand, ref, fetch.at[n])
        for n, (operand, ref) in enumerate(zip(operands, held))
    ]
    for copy in fetches:
        copy.start()
    steps(sizes, fetches, operands[5], *held, out_ref, *rest)


def steps(
    sizes,
    fetches,
    x_hbm,
    service,
    sources,
    levels,
    routes,
    owner,
    x_ref,
    phase_rates,
    batch_rates,
    out_ref,
    far,
    far_edge,
    far_left,
    near,
    mixed,
    high,
    low,
    conv,
    base,
    band,
    band_cat,
    leave,
    edge_one,
    edge_two,
    rim_one,
    rim_two,
    rim_mixed,
    picks,
    left_own,
    far_send,
    far_recv,
    far_edge_send,
    far_edge_recv,
    far_left_send,
    far_left_recv,
    near_send,
    near_recv,
    pick_send,
    pick_recv,
    edge_send,
    edge_recv,
):
    n_level, n_phase, masks, local_bits, cross = sizes
    singles = len(cross)
    C, S, Q, U, V = x_ref.shape
    halves = 2 if S > 1 else 1
    H = S // halves
    HU = H * U
    used = C * HU
    stride = high.shape[-1] // halves
    B = rim_one.shape[-2]
    G = rim_one.shape[-1] // (S * U)
    groups = Q // G
    lanes = G * S * U
    phases = n_phase * Q
    wide = 2 * B
    rim_at = 2 * C * S * Q
    bot_at = rim_at + groups * B
    bot_rows = (edge_one.shape[1] - bot_at) // C
    state_rows = 2 * C * Q
    rim_part = pl.ds(rim_at, edge_one.shape[1] - rim_at)
    parts = (
        [pl.ds(0, rim_at), rim_part],
        [pl.ds(s * state_rows, state_rows) for s in range(S)] + [rim_part],
    )
    level, src, phase = (lax.axis_index(n) for n in ("level", "src", "phase"))
    cores = [{"phase": lax.rem(phase + r, n_phase)} for r in range(1, n_phase)]
    fars = [{"src": jnp.bitwise_xor(src, m)} for m in masks]
    sides = ((1, level < n_level - 1, level > 0), (-1, level > 0, level < n_level - 1))

    barrier = pltpu.get_barrier_semaphore()
    for device in cores + fars:
        pl.semaphore_signal(barrier, inc=1, device_id=device, device_id_type=MESH)
    for toward, ahead, behind in sides:

        @pl.when(ahead)
        def _():
            pl.semaphore_signal(
                barrier, inc=1, device_id={"level": level + toward}, device_id_type=MESH
            )

    beside = (level > 0).astype(jnp.int32) + (level < n_level - 1).astype(jnp.int32)
    pl.semaphore_wait(barrier, len(cores) + len(fars) + beside)

    def make(source, target, sems, index, device):
        return pltpu.make_async_remote_copy(
            src_ref=source,
            dst_ref=target,
            send_sem=sems[0].at[index],
            recv_sem=sems[1].at[index],
            device_id=device,
            device_id_type=MESH,
        )

    def send(*parts):
        copy = make(*parts)
        copy.start()
        return copy

    def edge_copy(step, edge, part, way, h, block, toward):
        index = ((step * 2 + part) * 2 + way) * (n_level - 1) + h
        piece = edge.at[block, parts[step][part]]
        return make(piece, piece, (edge_send, edge_recv), index, {"level": level + toward})

    def hop(step, edge, part, way, h, act):
        toward, ahead, _ = sides[way]
        block = level - toward * h
        held = jnp.logical_and(block >= 0, block < n_level)

        @pl.when(jnp.logical_and(held, ahead))
        def _():
            act(edge_copy(step, edge, part, way, h, block, toward))

    def start_hop(step, edge, part):
        for way in range(2):
            hop(step, edge, part, way, 0, lambda copy: copy.start())

    def end_hop(step, edge, part, h):
        for way in range(2):
            toward = sides[way][0]
            block = level - toward * (h + 1)

            @pl.when(jnp.logical_and(block >= 0, block < n_level))
            def _():
                edge_copy(step, edge, part, way, h, block, -toward).wait_recv()

            if h < n_level - 2:
                hop(step, edge, part, way, h + 1, lambda copy: copy.start())

    def end_hops(step, edge, which, first, end):
        for h in range(first, min(end, n_level - 1)):
            for part in which:
                end_hop(step, edge, part, h)

    def end_sends(step, edge):
        for part in range(len(parts[step])):
            for h in range(n_level - 1):
                for way in range(2):
                    hop(step, edge, part, way, h, lambda copy: copy.wait_send())

    near_sems = (near_send, near_recv)
    x_near = [
        send(x_hbm, near.at[0, r], near_sems, r, device) for r, device in enumerate(cores)
    ]

    def send_far(s):
        return [
            send(x_hbm.at[:, s], far.at[m, :, s], (far_send, far_recv), m * S + s, device)
            for m, device in enumerate(fars)
        ]

    far_copies = [send_far(0)]
    for copy in fetches:
        copy.wait()

    for h in range(halves):
        if used < stride:
            gap = (phases, B + V, stride - used)
            high[:, :, h * stride + used : (h + 1) * stride] = jnp.zeros(gap, jnp.bfloat16)
            low[:, :, h * stride + used : (h + 1) * stride] = jnp.zeros(gap, jnp.bfloat16)

    tile_count = owner.shape[0]
    spots = []
    count = jnp.int32(0)
    for c in range(C):
        tile, filled = jnp.int32(0), jnp.int32(0)
        for t in range(tile_count):
            here = owner[t] == level * C + c
            tile = jnp.where(here, t, tile)
            filled = jnp.where(here, 1, filled)
        places = []
        for n in range(5):
            route = routes[tile, n]
            slot = owner[jnp.maximum(route, 0)]
            at = lax.div(slot, jnp.int32(C))
            places.append((route >= 0, at, slot - at * C))
        spots.append((places, levels[0, tile], levels[1, tile], filled))
        count = count + filled
    last = jnp.maximum(count - 1, 0)

    def turn(field, h, i, g):
        return field[:, h * H : (h + 1) * H, i * G + g].reshape(used, V).T

    def put(first, h, i, g, turned):
        top, rest = split(turned)
        high[first + i * G + g, B:, h * stride : h * stride + used] = top
        low[first + i * G + g, B:, h * stride : h * stride + used] = rest

    def group_lanes(turned, rows, c):
        return jnp.concatenate([t[rows, c * HU : (c + 1) * HU] for t in turned], axis=1)

    def keep_rims(rim, i, turned):
        for c in range(C):
            rim[c, i] = group_lanes(turned, slice(V - B, V), c)

    def keep_bots(edge, i, turned):
        for c in range(C):
            edge[level, pl.ds(bot_at + c * bot_rows + i, 1), :] = group_lanes(
                turned, slice(0, 1), c
            )

    def turn_all(field, i):
        return [turn(field, h, i, g) for h in range(halves) for g in range(G)]

    def keep_rows(edge, field, states):
        for s in states:
            for c in range(C):
                at = s * state_rows + c * Q
                edge[level, at : at + Q, :] = field[c, s, :, U - 1, :]
                at = at + C * Q
                edge[level, at : at + Q, :] = field[c, s, :, 0, :]

    def keep_last(edge, rim):
        edge[level, rim_at:bot_at, :] = rim[last].reshape(bot_at - rim_at, lanes)
        if bot_rows > groups:
            for c in range(C):
                at = bot_at + c * bot_rows
                edge[level, at + groups : at + bot_rows, :] = jnp.zeros(
                    (bot_rows - groups, lanes), jnp.float32
                )

    def turn_own(i, carry):
        turned = turn_all(x_ref, i)
        for h in range(halves):
            for g in range(G):
                put(0, h, i, g, turned[h * G + g])
        keep_rims(rim_one, i, turned)
        keep_bots(edge_one, i, turned)
        return carry

    keep_rows(edge_one, x_ref, range(S))
    start_hop(0, edge_one, 0)
    lax.fori_loop(0, groups, turn_own, 0)
    keep_last(edge_one, rim_one)
    start_hop(0, edge_one, 1)
    edge_copies = [
        send(
            edge_one.at[level, rim_part], far_edge.at[m], (far_edge_send, far_edge_recv), m, device
        )
        for m, device in enumerate(fars[:singles])
    ]
    far_copies += [send_far(s) for s in range(1, S)]

    across = lax.broadcasted_iota(jnp.int32, (phases, phases), 0) == lax.broadcasted_iota(
        jnp.int32, (phases, phases), 1
    )
    moving = jnp.where(across, 0.0, phase_rates[...])
    sums = moving
    for b in range(B):
        sums = sums + batch_rates[b]
    leaving = jnp.sum(sums, axis=1, keepdims=True)
    uniform = jnp.max(leaving) + service[0] + service[1]
    for k in range(SOURCES):
        uniform = uniform + jnp.maximum(sources[k, 2] + sources[k, 1], sources[k, 0])
    inverse = jnp.max(1.0 / jnp.full((8, 128), uniform, jnp.float32))
    leave[...] = jnp.broadcast_to(leaving * inverse, leave.shape)
    serve_one, serve_two = service[0] * inverse, service[1] * inverse
    turn_on = [sources[k, 0] * inverse for k in range(SOURCES)]
    turn_off = [sources[k, 1] * inverse for k in range(SOURCES)]
    arrive = [sources[k, 2] * inverse for k in range(SOURCES)]
    bit = {k: ((src >> (k - local_bits)) & 1) == 1 for k in cross}
    inflow = {k: jnp.where(bit[k], turn_on[k], turn_off[k]) for k in cross}
    outflow = {k: jnp.where(bit[k], turn_off[k], turn_on[k]) for k in cross}
    more_feed = {k: jnp.where(bit[k], -arrive[k], arrive[k]) for k in cross}
    feed, total_out = [], []
    for s in range(S):
        f = o = jnp.float32(0.0)
        for k in range(SOURCES):
            if k in cross:
                f = f + jnp.where(bit[k], arrive[k], 0.0)
                o = o + outflow[k]
            elif s >> k & 1:
                f, o = f + arrive[k], o + turn_off[k]
            else:
                o = o + turn_on[k]
        feed.append(f)
        total_out.append(o)
    twice = [2.0 * inflow[k] for k in cross]
    shift_in = [inflow[k] * more_feed[k] for k in cross]
    stay_in = [-inflow[k] * (more_feed[k] + inflow[k] - outflow[k]) for k in cross]
    back_in = jnp.float32(0.0)
    for k in cross:
        back_in = back_in + inflow[k] * outflow[k]
    pair_in = [
        2.0 * inflow[a] * inflow[b] for i, a in enumerate(cross) for b in cross[i + 1 :]
    ]

    base[...] = jnp.zeros(base.shape, jnp.float32)
    for r in range(n_phase):
        rank = lax.rem(phase + r, n_phase)
        at = pl.ds(pl.multiple_of(rank * Q, Q), Q)
        for w in range(B):
            base[pl.ds(r * Q * wide + w, Q, stride=wide), 0:phases] = (
                batch_rates[B - 1 - w, at, :] * inverse
            )
        row = lax.broadcasted_iota(jnp.int32, (Q, phases), 0) + rank * Q
        column = lax.broadcasted_iota(jnp.int32, (Q, phases), 1)
        base[pl.ds(r * Q * wide + B, Q, stride=wide), 0:phases] = (
            jnp.where(row == column, 0.0, phase_rates[at, :]) * inverse
        )
    out_rows = base[...].T
    base_two = jnp.zeros((Q, phases * wide), jnp.float32)
    for r in range(n_phase):
        base_two = jnp.where(phase == r, out_rows[r * Q : (r + 1) * Q], base_two)
    for v in range(B):
        band[:, v, :] = pltpu.roll(base_two, v, 1) if v else base_two
    M = Q * B
    band_high, band_low = split(band[...].reshape(M, phases * wide))
    band_cat[0:M, :] = band_high
    band_cat[M:, :] = band_low

    def multiply(v, carry):
        window = pl.ds(pl.multiple_of(v * B, B), wide)
        top = high[:, window, :].reshape(phases * wide, halves * stride)
        rest = low[:, window, :].reshape(phases * wide, halves * stride)
        both = jnp.dot(band_cat[...], top, preferred_element_type=jnp.float32)
        third = jnp.dot(band_cat[0:M, :], rest, preferred_element_type=jnp.float32)
        total = both[0:M] + (both[M:] + third)
        conv[:, pl.ds(pl.multiple_of(v * B, B), B), :] = total.reshape(Q, B, halves * stride)
        return carry

    def turn_near(step, which):
        for r in range(n_phase - 1):

            def one(i, carry):
                for h in which:
                    for g in range(G):
                        put((r + 1) * Q, h, i, g, turn(near.at[step, r], h, i, g))
                return carry

            lax.fori_loop(0, groups, one, 0)

    def by_half(values, h, g):
        at = (h * G + g) * HU
        return jnp.concatenate([v[:, at : at + HU] for v in values], axis=1)

    def spread(i, first, values):
        for h in range(halves):
            for g in range(G):
                top, rest = split(by_half(values, h, g))
                high[first + i * G + g, 0:B, h * stride : h * stride + used] = top
                low[first + i * G + g, 0:B, h * stride : h * stride + used] = rest

    def take_rims(step, edge, rim):
        def pick(i, carry):
            values = []
            for c in range(C):
                there, at, _ = spots[c][0][0]
                if c == 0:
                    found = edge[at, pl.ds(pl.multiple_of(rim_at + i * B, 8), B), :]
                else:
                    found = rim[c - 1, i]
                value = jnp.where(there, found, 0.0)
                picks[step, 0, c, i] = value
                values.append(value)
            spread(i, 0, values)
            return carry

        lax.fori_loop(0, groups, pick, 0)
        return [
            send(
                picks.at[step, 0],
                picks.at[step, r + 1],
                (pick_send, pick_recv),
                step * (n_phase - 1) + r,
                device,
            )
            for r, device in enumerate(cores)
        ]

    def share_rims(step, copies):
        for r, copy in enumerate(copies):
            copy.wait_recv()

            def take(i, carry):
                spread(i, (r + 1) * Q, [picks[step, r + 1, c, i] for c in range(C)])
                return carry

            lax.fori_loop(0, groups, take, 0)

    def add_above(edge):
        def one(i, carry):
            lane = lax.broadcasted_iota(jnp.int32, (8, lanes), 1)
            values = []
            for c in range(C):
                rolled = []
                for n, amount in ((1, 1), (4, lanes - (U - 1))):
                    there, at, slot = spots[c][0][n]
                    found = edge[at, pl.ds(bot_at + slot * bot_rows + i, 1), :]
                    found = jnp.broadcast_to(jnp.where(there, found, 0.0), (8, lanes))
                    rolled.append(pltpu.roll(found, amount, 1))
                values.append(jnp.where(lane % U == 0, rolled[1], rolled[0]))
            for h in range(halves):
                part = slice(h * stride, h * stride + used)
                for g in range(G):
                    whole = by_half(values, h, g)
                    q = i * G + g
                    conv[q, V - 1 : V, part] = conv[q, V - 1 : V, part] + serve_one * whole[0:1]
            return carry

        lax.fori_loop(0, groups, one, 0)

    def beside(edge, place, kind, s):
        there, at, slot = place
        first = s * state_rows + kind * C * Q
        return jnp.where(there, edge[at, pl.ds(first + slot * Q, Q), :], 0.0)

    def gone_from(c, q, line, lane):
        _, level_one, level_two, _ = spots[c]
        return (
            leave[pl.ds(phase * Q + q, 1), :]
            + jnp.where(level_one * V + lane > 0, serve_one, 0.0)
            + jnp.where(level_two * U + line > 0, serve_two, 0.0)
        )

    def within(s, here, gone, line, lane):
        before = jnp.where(line == 0, 0.0, pltpu.roll(here, 1, 0))
        after = jnp.where(line == U - 1, 0.0, pltpu.roll(here, U - 1, 0))
        moved = jnp.where(lane == V - 1, 0.0, pltpu.roll(before, V - 1, 1))
        value = here - (gone + (feed[s] + total_out[s])) * here
        return value + serve_one * moved + serve_two * after + feed[s] * before

    def flip_rate(s, k):
        return turn_on[k] if s >> k & 1 else turn_off[k]

    def combine(step, field, result):
        def one(q, carry):
            line = lax.broadcasted_iota(jnp.int32, (U, V), 0)
            lane = lax.broadcasted_iota(jnp.int32, (U, V), 1)
            for c in range(C):
                gone = gone_from(c, q, line, lane)
                blocks = [field[c, s, q] for s in range(S)]
                for s in range(S):
                    value = within(s, blocks[s], gone, line, lane)
                    for k in range(local_bits):
                        value = value + flip_rate(s, k) * blocks[s ^ (1 << k)]
                    if step == 1 and singles:
                        value = value + back_in * x_ref[c, s, q]
                    result[c, s, q] = value
            return carry

        lax.fori_loop(0, Q, one, 0)

    def add_far(s):
        def one(q, carry):
            for c in range(C):
                value = mixed[c, s, q]
                for k in range(singles):
                    value = value + twice[k] * far[k, c, s, q]
                mixed[c, s, q] = value
            return carry

        lax.fori_loop(0, Q, one, 0)

    def combine_far(s):
        def one(q, carry):
            line = lax.broadcasted_iota(jnp.int32, (U, V), 0)
            lane = lax.broadcasted_iota(jnp.int32, (U, V), 1)
            for c in range(C):
                here = shifted = stay = jnp.zeros((U, V), jnp.float32)
                for k in range(singles):
                    other = far[k, c, s, q]
                    here = here + twice[k] * other
                    shifted = shifted + shift_in[k] * other
                    stay = stay + stay_in[k] * other
                for k in range(singles, len(masks)):
                    stay = stay + pair_in[k - singles] * far[k, c, s, q]
                value = within(s, here, gone_from(c, q, line, lane), line, lane) + stay
                value = value + jnp.where(line == 0, 0.0, pltpu.roll(shifted, 1, 0))
                out_ref[c, s, q] = out_ref[c, s, q] + value
                for k in range(local_bits):
                    t = s ^ (1 << k)
                    out_ref[c, t, q] = out_ref[c, t, q] + flip_rate(t, k) * here
            return carry

        lax.fori_loop(0, Q, one, 0)

    def add_rows(step, edge, result):
        lane = lax.broadcasted_iota(jnp.int32, (Q, V), 1)
        for c in range(C):
            places = spots[c][0]
            for s in range(S):
                left = beside(edge, places[2], 0, s)
                right = beside(edge, places[3], 1, s)
                moved = jnp.where(lane == V - 1, 0.0, pltpu.roll(left, V - 1, 1))
                added = feed[s] * left + serve_one * moved
                if step == 1:
                    for k in range(singles):
                        added = added + shift_in[k] * far_left[k, c, s * Q : (s + 1) * Q, :]
                result[c, s, :, 0, :] = result[c, s, :, 0, :] + added
                result[c, s, :, U - 1, :] = result[c, s, :, U - 1, :] + serve_two * right

    def finish(step, result):
        def one(q, carry):
            for h in range(halves):
                back = conv[q, :, h * stride : (h + 1) * stride].T[0:used].reshape(C, H, U, V)
                for c in range(C):
                    value = result[c, h * H : (h + 1) * H, q] + back[c]
                    if step == 1:
                        value = jnp.where(spots[c][3] > 0, value, 0.0)
                    result[c, h * H : (h + 1) * H, q] = value
            return carry

        lax.fori_loop(0, Q, one, 0)

    end_hops(0, edge_one, range(2), 0, 1)
    for copy in x_near:
        copy.wait_recv()
    turn_near(0, range(halves))
    combine(0, x_ref, mixed)
    end_hops(0, edge_one, range(2), 1, 2)
    lax.fori_loop(1, V // B, multiply, 0)
    end_hops(0, edge_one, range(2), 2, n_level)
    pick_copies = take_rims(0, edge_one, rim_one)
    add_above(edge_one)
    add_rows(0, edge_one, mixed)
    share_rims(0, pick_copies)
    multiply(0, 0)
    finish(0, mixed)

    def turn_edges(i, carry):
        for c in range(C):
            pieces = [
                mixed[c, h * H : (h + 1) * H, i * G + g].reshape(HU, V)
                for h in range(halves)
                for g in range(G)
            ]
            turned = jnp.concatenate(pieces, axis=0).T
            rim_mixed[c, i] = turned[V - B :]
            edge_two[level, pl.ds(bot_at + c * bot_rows + i, 1), :] = turned[0:1]
        return carry

    lax.fori_loop(0, groups, turn_edges, 0)
    keep_last(edge_two, rim_mixed)
    for k, copy in enumerate(edge_copies):
        copy.wait_recv()
        edge_two[level, rim_part] = edge_two[level, rim_part] + twice[k] * far_edge[k]
    start_hop(1, edge_two, S)

    for c in range(C):
        for s in range(S):
            left_own[c, s * Q : (s + 1) * Q, :] = beside(edge_one, spots[c][0][2], 0, s)
    left_copies = [
        send(left_own, far_left.at[m], (far_left_send, far_left_recv), m, device)
        for m, device in enumerate(fars[:singles])
    ]

    combine(1, mixed, out_ref)
    end_hops(1, edge_two, [S], 0, 1)

    def turn_mixed(h):
        def one(i, carry):
            for g in range(G):
                turned = turn(mixed, h, i, g)
                put(0, h, i, g, turned)
                for c in range(C):
                    at = (h * G + g) * HU
                    rim_two[c, i, :, at : at + HU] = turned[V - B :, c * HU : (c + 1) * HU]
            return carry

        lax.fori_loop(0, groups, one, 0)

    mixed_near = []
    for s in range(S):
        for copy in far_copies[s]:
            copy.wait_recv()
        add_far(s)
        fresh = []
        for r, device in enumerate(cores):
            index = (n_phase - 1) * (1 + s) + r
            fresh.append(send(mixed.at[:, s], near.at[1, r, :, s], near_sems, index, device))
        mixed_near += fresh
        keep_rows(edge_two, mixed, [s])
        start_hop(1, edge_two, s)
        end_hops(1, edge_two, [s - 1 if s else S], 1, 2)
        if s == S - 1:
            turn_mixed(halves - 1)
        combine_far(s)
        end_hops(1, edge_two, [s], 0, 1)
        for copy in fresh:
            copy.wait_recv()
        if (s + 1) % H == 0:
            if s < S - 1:
                turn_mixed(s // H)
            turn_near(1, [s // H])
    end_hops(1, edge_two, [S - 1], 1, 2)
    lax.fori_loop(1, V // B, multiply, 0)
    end_hops(1, edge_two, range(S + 1), 2, n_level)
    last_picks = take_rims(1, edge_two, rim_two)
    pick_copies += last_picks
    add_above(edge_two)
    for copy in left_copies:
        copy.wait_recv()
    add_rows(1, edge_two, out_ref)
    share_rims(1, last_picks)
    multiply(0, 0)
    finish(1, out_ref)

    for copy in x_near + mixed_near + pick_copies + left_copies + edge_copies:
        copy.wait_send()
    for copies in far_copies:
        for copy in copies:
            copy.wait_send()
    end_sends(0, edge_one)
    end_sends(1, edge_two)


def body(
    n_level,
    n_phase,
    state_values,
    phase_rates,
    batch_rates,
    service_rates,
    source_rates,
    tile_levels,
    routes,
    tile_owner,
):
    C, S, Q, U, V = state_values.shape
    phases = phase_rates.shape[0]
    batch = batch_rates.shape[0]
    local_bits = S.bit_length() - 1
    cross = list(range(local_bits, SOURCES))
    masks = [1 << (k - local_bits) for k in cross]
    masks += [masks[i] | masks[j] for i in range(len(cross)) for j in range(i + 1, len(cross))]
    group = min(Q, max(1, 128 // (S * U)))
    lanes = group * S * U
    groups = Q // group
    halves = 2 if S > 1 else 1
    width = halves * (-(-(C * S * U // halves) // 128) * 128)
    edge_rows = groups * batch + 2 * C * S * Q + C * (-(-groups // 8) * 8)
    f32, bf16 = jnp.float32, jnp.bfloat16
    vmem = pl.BlockSpec(memory_space=pltpu.VMEM)
    singles, fars, cores = max(1, len(cross)), max(1, len(masks)), max(1, n_phase - 1)
    counts = [fars * S, singles, singles, cores * (1 + S), 2 * cores, max(1, (6 + 2 * S) * (n_level - 1))]
    shapes = [
        ((fars,) + state_values.shape, f32),
        ((singles, edge_rows - 2 * C * S * Q, lanes), f32),
        ((singles, C, S * Q, V), f32),
        ((2, cores) + state_values.shape, f32),
        (state_values.shape, f32),
        ((phases, batch + V, width), bf16),
        ((phases, batch + V, width), bf16),
        ((Q, V, width), f32),
        ((phases * 2 * batch, 128), f32),
        ((Q, batch, phases * 2 * batch), f32),
        ((2 * Q * batch, phases * 2 * batch), bf16),
        ((phases, V), f32),
        ((n_level, edge_rows, lanes), f32),
        ((n_level, edge_rows, lanes), f32),
        ((C, groups, batch, lanes), f32),
        ((C, groups, batch, lanes), f32),
        ((C, groups, batch, lanes), f32),
        ((2, n_phase, C, groups, batch, lanes), f32),
        ((C, S * Q, V), f32),
    ]
    operands = (
        service_rates,
        source_rates,
        tile_levels.T,
        routes,
        tile_owner,
        state_values,
        phase_rates,
        batch_rates,
    )
    return pl.pallas_call(
        functools.partial(kernel, (n_level, n_phase, masks, local_bits, cross)),
        out_shape=jax.ShapeDtypeStruct(state_values.shape, f32),
        in_specs=[pl.BlockSpec(memory_space=pl.ANY)] * 8,
        out_specs=vmem,
        scratch_shapes=[pltpu.SMEM(a.shape, a.dtype) for a in operands[:5]]
        + [pltpu.VMEM(a.shape, a.dtype) for a in operands[5:]]
        + [pltpu.SemaphoreType.DMA((len(operands),))]
        + [pltpu.VMEM(*shape) for shape in shapes]
        + [pltpu.SemaphoreType.DMA((n,)) for n in counts for _ in range(2)],
        compiler_params=pltpu.CompilerParams(
            collective_id=0, has_side_effects=True, vmem_limit_bytes=60 * 1024 * 1024
        ),
    )(*operands)


def solution(mesh):
    placed = (
        P(("groups", "level"), "src", "phase", None, None),
        P("groups", None),
        P("groups", None, None),
        P("groups"),
        P("groups", None),
        P("groups", None),
        P("groups", None),
        P("groups"),
    )
    axes = mesh.shape
    return jax.shard_map(
        functools.partial(body, axes["level"], axes["phase"]),
        mesh=mesh,
        in_specs=placed,
        out_specs=P(("groups", "level"), "src", "phase", None, None),
        check_vma=False,
    )
```

```python
import functools

import jax
import jax.numpy as jnp
from jax import lax
from jax.experimental import pallas as pl
from jax.experimental.pallas import tpu as pltpu
from jax.sharding import PartitionSpec as P

SOURCES = 3
MESH = pl.DeviceIdType.MESH


def split(values):
    high = values.astype(jnp.bfloat16)
    low = (values - high.astype(jnp.float32)).astype(jnp.bfloat16)
    return high, low


def kernel(
    sizes,
    *refs,
):
    operands, out_ref, held, fetch, rest = refs[:8], refs[8], refs[9:17], refs[17], refs[18:]
    fetches = [
        pltpu.make_async_copy(operand, ref, fetch.at[n])
        for n, (operand, ref) in enumerate(zip(operands, held))
    ]
    for copy in fetches:
        copy.start()
    steps(sizes, fetches, operands[5], *held, out_ref, *rest)


def steps(
    sizes,
    fetches,
    x_hbm,
    service,
    sources,
    levels,
    routes,
    owner,
    x_ref,
    phase_rates,
    batch_rates,
    out_ref,
    far,
    far_edge,
    far_left,
    near,
    mixed,
    high,
    low,
    conv,
    base,
    band,
    band_cat,
    leave,
    edge_one,
    edge_two,
    rim_one,
    rim_two,
    rim_mixed,
    picks,
    left_own,
    far_send,
    far_recv,
    far_edge_send,
    far_edge_recv,
    far_left_send,
    far_left_recv,
    near_send,
    near_recv,
    pick_send,
    pick_recv,
    edge_send,
    edge_recv,
):
    n_level, n_phase, masks, local_bits, cross = sizes
    singles = len(cross)
    C, S, Q, U, V = x_ref.shape
    halves = 2 if S > 1 else 1
    H = S // halves
    HU = H * U
    used = C * HU
    stride = high.shape[-1] // halves
    B = rim_one.shape[-2]
    G = rim_one.shape[-1] // (S * U)
    groups = Q // G
    lanes = G * S * U
    phases = n_phase * Q
    wide = 2 * B
    low_at = 0
    up_at = C * S * Q
    rim_at = 2 * C * S * Q
    bot_at = rim_at + groups * B
    bot_rows = (edge_one.shape[1] - bot_at) // C
    parts = (pl.ds(0, rim_at), pl.ds(rim_at, edge_one.shape[1] - rim_at))
    level, src, phase = (lax.axis_index(n) for n in ("level", "src", "phase"))
    cores = [{"phase": lax.rem(phase + r, n_phase)} for r in range(1, n_phase)]
    fars = [{"src": jnp.bitwise_xor(src, m)} for m in masks]
    sides = ((1, level < n_level - 1, level > 0), (-1, level > 0, level < n_level - 1))

    barrier = pltpu.get_barrier_semaphore()
    for device in cores + fars:
        pl.semaphore_signal(barrier, inc=1, device_id=device, device_id_type=MESH)
    for toward, ahead, behind in sides:

        @pl.when(ahead)
        def _():
            pl.semaphore_signal(
                barrier, inc=1, device_id={"level": level + toward}, device_id_type=MESH
            )

    beside = (level > 0).astype(jnp.int32) + (level < n_level - 1).astype(jnp.int32)
    pl.semaphore_wait(barrier, len(cores) + len(fars) + beside)

    def make(source, target, sems, index, device):
        return pltpu.make_async_remote_copy(
            src_ref=source,
            dst_ref=target,
            send_sem=sems[0].at[index],
            recv_sem=sems[1].at[index],
            device_id=device,
            device_id_type=MESH,
        )

    def send(*parts):
        copy = make(*parts)
        copy.start()
        return copy

    def edge_copy(step, edge, part, way, h, block, toward):
        index = ((step * 2 + part) * 2 + way) * (n_level - 1) + h
        piece = edge.at[block, parts[part]]
        return make(piece, piece, (edge_send, edge_recv), index, {"level": level + toward})

    def hop(step, edge, part, way, h, act):
        toward, ahead, _ = sides[way]
        block = level - toward * h
        held = jnp.logical_and(block >= 0, block < n_level)

        @pl.when(jnp.logical_and(held, ahead))
        def _():
            act(edge_copy(step, edge, part, way, h, block, toward))

    def start_hop(step, edge, part):
        for way in range(2):
            hop(step, edge, part, way, 0, lambda copy: copy.start())

    def end_hop(step, edge, part, h):
        for way in range(2):
            toward = sides[way][0]
            block = level - toward * (h + 1)

            @pl.when(jnp.logical_and(block >= 0, block < n_level))
            def _():
                edge_copy(step, edge, part, way, h, block, -toward).wait_recv()

            if h < n_level - 2:
                hop(step, edge, part, way, h + 1, lambda copy: copy.start())

    def end_hops(step, edge, first, end):
        for h in range(first, min(end, n_level - 1)):
            for part in range(2):
                end_hop(step, edge, part, h)

    def end_sends(step, edge):
        for part in range(2):
            for h in range(n_level - 1):
                for way in range(2):
                    hop(step, edge, part, way, h, lambda copy: copy.wait_send())

    near_sems = (near_send, near_recv)
    x_near = [
        send(x_hbm, near.at[0, r], near_sems, r, device) for r, device in enumerate(cores)
    ]

    def send_far(s):
        return [
            send(x_hbm.at[:, s], far.at[m, :, s], (far_send, far_recv), m * S + s, device)
            for m, device in enumerate(fars)
        ]

    far_copies = [send_far(0)]
    for copy in fetches:
        copy.wait()

    for h in range(halves):
        if used < stride:
            gap = (phases, B + V, stride - used)
            high[:, :, h * stride + used : (h + 1) * stride] = jnp.zeros(gap, jnp.bfloat16)
            low[:, :, h * stride + used : (h + 1) * stride] = jnp.zeros(gap, jnp.bfloat16)

    tile_count = owner.shape[0]
    spots = []
    count = jnp.int32(0)
    for c in range(C):
        tile, filled = jnp.int32(0), jnp.int32(0)
        for t in range(tile_count):
            here = owner[t] == level * C + c
            tile = jnp.where(here, t, tile)
            filled = jnp.where(here, 1, filled)
        places = []
        for n in range(5):
            route = routes[tile, n]
            slot = owner[jnp.maximum(route, 0)]
            at = lax.div(slot, jnp.int32(C))
            places.append((route >= 0, at, slot - at * C))
        spots.append((places, levels[0, tile], levels[1, tile], filled))
        count = count + filled
    last = jnp.maximum(count - 1, 0)

    def turn(field, h, i, g):
        return field[:, h * H : (h + 1) * H, i * G + g].reshape(used, V).T

    def put(first, h, i, g, turned):
        top, rest = split(turned)
        high[first + i * G + g, B:, h * stride : h * stride + used] = top
        low[first + i * G + g, B:, h * stride : h * stride + used] = rest

    def group_lanes(turned, rows, c):
        return jnp.concatenate([t[rows, c * HU : (c + 1) * HU] for t in turned], axis=1)

    def keep_rims(rim, i, turned):
        for c in range(C):
            rim[c, i] = group_lanes(turned, slice(V - B, V), c)

    def keep_bots(edge, i, turned):
        for c in range(C):
            edge[level, pl.ds(bot_at + c * bot_rows + i, 1), :] = group_lanes(
                turned, slice(0, 1), c
            )

    def turn_all(field, i):
        return [turn(field, h, i, g) for h in range(halves) for g in range(G)]

    def keep_rows(edge, field):
        for c in range(C):
            for s in range(S):
                at = (c * S + s) * Q
                edge[level, low_at + at : low_at + at + Q, :] = field[c, s, :, U - 1, :]
                edge[level, up_at + at : up_at + at + Q, :] = field[c, s, :, 0, :]

    def keep_last(edge, rim):
        edge[level, rim_at:bot_at, :] = rim[last].reshape(bot_at - rim_at, lanes)
        if bot_rows > groups:
            for c in range(C):
                at = bot_at + c * bot_rows
                edge[level, at + groups : at + bot_rows, :] = jnp.zeros(
                    (bot_rows - groups, lanes), jnp.float32
                )

    def turn_own(i, carry):
        turned = turn_all(x_ref, i)
        for h in range(halves):
            for g in range(G):
                put(0, h, i, g, turned[h * G + g])
        keep_rims(rim_one, i, turned)
        keep_bots(edge_one, i, turned)
        return carry

    keep_rows(edge_one, x_ref)
    start_hop(0, edge_one, 0)
    lax.fori_loop(0, groups, turn_own, 0)
    keep_last(edge_one, rim_one)
    start_hop(0, edge_one, 1)
    edge_copies = [
        send(edge_one.at[level], far_edge.at[m], (far_edge_send, far_edge_recv), m, device)
        for m, device in enumerate(fars[:singles])
    ]
    far_copies += [send_far(s) for s in range(1, S)]

    across = lax.broadcasted_iota(jnp.int32, (phases, phases), 0) == lax.broadcasted_iota(
        jnp.int32, (phases, phases), 1
    )
    moving = jnp.where(across, 0.0, phase_rates[...])
    sums = moving
    for b in range(B):
        sums = sums + batch_rates[b]
    leaving = jnp.sum(sums, axis=1, keepdims=True)
    uniform = jnp.max(leaving) + service[0] + service[1]
    for k in range(SOURCES):
        uniform = uniform + jnp.maximum(sources[k, 2] + sources[k, 1], sources[k, 0])
    inverse = jnp.max(1.0 / jnp.full((8, 128), uniform, jnp.float32))
    leave[...] = jnp.broadcast_to(leaving * inverse, leave.shape)
    serve_one, serve_two = service[0] * inverse, service[1] * inverse
    turn_on = [sources[k, 0] * inverse for k in range(SOURCES)]
    turn_off = [sources[k, 1] * inverse for k in range(SOURCES)]
    arrive = [sources[k, 2] * inverse for k in range(SOURCES)]
    bit = {k: ((src >> (k - local_bits)) & 1) == 1 for k in cross}
    inflow = {k: jnp.where(bit[k], turn_on[k], turn_off[k]) for k in cross}
    outflow = {k: jnp.where(bit[k], turn_off[k], turn_on[k]) for k in cross}
    more_feed = {k: jnp.where(bit[k], -arrive[k], arrive[k]) for k in cross}
    feed, total_out = [], []
    for s in range(S):
        f = o = jnp.float32(0.0)
        for k in range(SOURCES):
            if k in cross:
                f = f + jnp.where(bit[k], arrive[k], 0.0)
                o = o + outflow[k]
            elif s >> k & 1:
                f, o = f + arrive[k], o + turn_off[k]
            else:
                o = o + turn_on[k]
        feed.append(f)
        total_out.append(o)
    twice = [2.0 * inflow[k] for k in cross]
    shift_in = [inflow[k] * more_feed[k] for k in cross]
    stay_in = [-inflow[k] * (more_feed[k] + inflow[k] - outflow[k]) for k in cross]
    back_in = jnp.float32(0.0)
    for k in cross:
        back_in = back_in + inflow[k] * outflow[k]
    pair_in = [
        2.0 * inflow[a] * inflow[b] for i, a in enumerate(cross) for b in cross[i + 1 :]
    ]

    base[...] = jnp.zeros(base.shape, jnp.float32)
    for r in range(n_phase):
        rank = lax.rem(phase + r, n_phase)
        at = pl.ds(pl.multiple_of(rank * Q, Q), Q)
        for w in range(B):
            base[pl.ds(r * Q * wide + w, Q, stride=wide), 0:phases] = (
                batch_rates[B - 1 - w, at, :] * inverse
            )
        row = lax.broadcasted_iota(jnp.int32, (Q, phases), 0) + rank * Q
        column = lax.broadcasted_iota(jnp.int32, (Q, phases), 1)
        base[pl.ds(r * Q * wide + B, Q, stride=wide), 0:phases] = (
            jnp.where(row == column, 0.0, phase_rates[at, :]) * inverse
        )
    out_rows = base[...].T
    base_two = jnp.zeros((Q, phases * wide), jnp.float32)
    for r in range(n_phase):
        base_two = jnp.where(phase == r, out_rows[r * Q : (r + 1) * Q], base_two)
    for v in range(B):
        band[:, v, :] = pltpu.roll(base_two, v, 1) if v else base_two
    M = Q * B
    band_high, band_low = split(band[...].reshape(M, phases * wide))
    band_cat[0:M, :] = band_high
    band_cat[M:, :] = band_low

    def multiply(v, carry):
        window = pl.ds(pl.multiple_of(v * B, B), wide)
        top = high[:, window, :].reshape(phases * wide, halves * stride)
        rest = low[:, window, :].reshape(phases * wide, halves * stride)
        both = jnp.dot(band_cat[...], top, preferred_element_type=jnp.float32)
        third = jnp.dot(band_cat[0:M, :], rest, preferred_element_type=jnp.float32)
        total = both[0:M] + (both[M:] + third)
        conv[:, pl.ds(pl.multiple_of(v * B, B), B), :] = total.reshape(Q, B, halves * stride)
        return carry

    def turn_near(step, which):
        for r in range(n_phase - 1):

            def one(i, carry):
                for h in which:
                    for g in range(G):
                        put((r + 1) * Q, h, i, g, turn(near.at[step, r], h, i, g))
                return carry

            lax.fori_loop(0, groups, one, 0, unroll=2)

    def by_half(values, h, g):
        at = (h * G + g) * HU
        return jnp.concatenate([v[:, at : at + HU] for v in values], axis=1)

    def spread(i, first, values):
        for h in range(halves):
            for g in range(G):
                top, rest = split(by_half(values, h, g))
                high[first + i * G + g, 0:B, h * stride : h * stride + used] = top
                low[first + i * G + g, 0:B, h * stride : h * stride + used] = rest

    def take_rims(step, edge, rim):
        def pick(i, carry):
            values = []
            for c in range(C):
                there, at, _ = spots[c][0][0]
                if c == 0:
                    found = edge[at, pl.ds(pl.multiple_of(rim_at + i * B, 8), B), :]
                else:
                    found = rim[c - 1, i]
                value = jnp.where(there, found, 0.0)
                picks[step, 0, c, i] = value
                values.append(value)
            spread(i, 0, values)
            return carry

        lax.fori_loop(0, groups, pick, 0)
        return [
            send(
                picks.at[step, 0],
                picks.at[step, r + 1],
                (pick_send, pick_recv),
                step * (n_phase - 1) + r,
                device,
            )
            for r, device in enumerate(cores)
        ]

    def share_rims(step, copies):
        for r, copy in enumerate(copies):
            copy.wait_recv()

            def take(i, carry):
                spread(i, (r + 1) * Q, [picks[step, r + 1, c, i] for c in range(C)])
                return carry

            lax.fori_loop(0, groups, take, 0)

    def add_above(edge):
        def one(i, carry):
            lane = lax.broadcasted_iota(jnp.int32, (8, lanes), 1)
            values = []
            for c in range(C):
                rolled = []
                for n, amount in ((1, 1), (4, lanes - (U - 1))):
                    there, at, slot = spots[c][0][n]
                    found = edge[at, pl.ds(bot_at + slot * bot_rows + i, 1), :]
                    found = jnp.broadcast_to(jnp.where(there, found, 0.0), (8, lanes))
                    rolled.append(pltpu.roll(found, amount, 1))
                values.append(jnp.where(lane % U == 0, rolled[1], rolled[0]))
            for h in range(halves):
                part = slice(h * stride, h * stride + used)
                for g in range(G):
                    whole = by_half(values, h, g)
                    q = i * G + g
                    conv[q, V - 1 : V, part] = conv[q, V - 1 : V, part] + serve_one * whole[0:1]
            return carry

        lax.fori_loop(0, groups, one, 0)

    def beside(edge, place, first, s):
        there, at, slot = place
        return jnp.where(there, edge[at, pl.ds(first + (slot * S + s) * Q, Q), :], 0.0)

    def gone_from(c, q, line, lane):
        _, level_one, level_two, _ = spots[c]
        return (
            leave[pl.ds(phase * Q + q, 1), :]
            + jnp.where(level_one * V + lane > 0, serve_one, 0.0)
            + jnp.where(level_two * U + line > 0, serve_two, 0.0)
        )

    def within(s, here, gone, line, lane):
        before = jnp.where(line == 0, 0.0, pltpu.roll(here, 1, 0))
        after = jnp.where(line == U - 1, 0.0, pltpu.roll(here, U - 1, 0))
        moved = jnp.where(lane == V - 1, 0.0, pltpu.roll(before, V - 1, 1))
        value = here - (gone + (feed[s] + total_out[s])) * here
        return value + serve_one * moved + serve_two * after + feed[s] * before

    def flip_rate(s, k):
        return turn_on[k] if s >> k & 1 else turn_off[k]

    def combine(step, field, result):
        def one(q, carry):
            line = lax.broadcasted_iota(jnp.int32, (U, V), 0)
            lane = lax.broadcasted_iota(jnp.int32, (U, V), 1)
            for c in range(C):
                gone = gone_from(c, q, line, lane)
                blocks = [field[c, s, q] for s in range(S)]
                for s in range(S):
                    value = within(s, blocks[s], gone, line, lane)
                    for k in range(local_bits):
                        value = value + flip_rate(s, k) * blocks[s ^ (1 << k)]
                    if step == 1 and singles:
                        value = value + back_in * x_ref[c, s, q]
                    result[c, s, q] = value
            return carry

        lax.fori_loop(0, Q, one, 0)

    def add_far(s):
        def one(q, carry):
            for c in range(C):
                value = mixed[c, s, q]
                for k in range(singles):
                    value = value + twice[k] * far[k, c, s, q]
                mixed[c, s, q] = value
            return carry

        lax.fori_loop(0, Q, one, 0, unroll=2)

    def combine_far(s):
        def one(q, carry):
            line = lax.broadcasted_iota(jnp.int32, (U, V), 0)
            lane = lax.broadcasted_iota(jnp.int32, (U, V), 1)
            for c in range(C):
                here = shifted = stay = jnp.zeros((U, V), jnp.float32)
                for k in range(singles):
                    other = far[k, c, s, q]
                    here = here + twice[k] * other
                    shifted = shifted + shift_in[k] * other
                    stay = stay + stay_in[k] * other
                for k in range(singles, len(masks)):
                    stay = stay + pair_in[k - singles] * far[k, c, s, q]
                value = within(s, here, gone_from(c, q, line, lane), line, lane) + stay
                value = value + jnp.where(line == 0, 0.0, pltpu.roll(shifted, 1, 0))
                out_ref[c, s, q] = out_ref[c, s, q] + value
                for k in range(local_bits):
                    t = s ^ (1 << k)
                    out_ref[c, t, q] = out_ref[c, t, q] + flip_rate(t, k) * here
            return carry

        lax.fori_loop(0, Q, one, 0)

    def add_rows(step, edge, result):
        lane = lax.broadcasted_iota(jnp.int32, (Q, V), 1)
        for c in range(C):
            places = spots[c][0]
            for s in range(S):
                left = beside(edge, places[2], low_at, s)
                right = beside(edge, places[3], up_at, s)
                moved = jnp.where(lane == V - 1, 0.0, pltpu.roll(left, V - 1, 1))
                added = feed[s] * left + serve_one * moved
                if step == 1:
                    for k in range(singles):
                        added = added + shift_in[k] * far_left[k, c, s * Q : (s + 1) * Q, :]
                result[c, s, :, 0, :] = result[c, s, :, 0, :] + added
                result[c, s, :, U - 1, :] = result[c, s, :, U - 1, :] + serve_two * right

    def finish(step, result):
        def one(q, carry):
            for h in range(halves):
                back = conv[q, :, h * stride : (h + 1) * stride].T[0:used].reshape(C, H, U, V)
                for c in range(C):
                    value = result[c, h * H : (h + 1) * H, q] + back[c]
                    if step == 1:
                        value = jnp.where(spots[c][3] > 0, value, 0.0)
                    result[c, h * H : (h + 1) * H, q] = value
            return carry

        lax.fori_loop(0, Q, one, 0, unroll=2)

    end_hops(0, edge_one, 0, 1)
    for copy in x_near:
        copy.wait_recv()
    turn_near(0, range(halves))
    combine(0, x_ref, mixed)
    end_hops(0, edge_one, 1, 2)
    lax.fori_loop(1, V // B, multiply, 0)
    end_hops(0, edge_one, 2, n_level)
    pick_copies = take_rims(0, edge_one, rim_one)
    add_above(edge_one)
    add_rows(0, edge_one, mixed)
    share_rims(0, pick_copies)
    multiply(0, 0)
    finish(0, mixed)

    def add_far_edges(part):
        for k in range(singles):
            edge_two[level, parts[part]] = (
                edge_two[level, parts[part]] + twice[k] * far_edge[k, parts[part]]
            )
        start_hop(1, edge_two, part)

    keep_rows(edge_two, mixed)
    for copy in edge_copies:
        copy.wait_recv()
    add_far_edges(0)

    def turn_edges(i, carry):
        for c in range(C):
            pieces = [
                mixed[c, h * H : (h + 1) * H, i * G + g].reshape(HU, V)
                for h in range(halves)
                for g in range(G)
            ]
            turned = jnp.concatenate(pieces, axis=0).T
            rim_mixed[c, i] = turned[V - B :]
            edge_two[level, pl.ds(bot_at + c * bot_rows + i, 1), :] = turned[0:1]
        return carry

    lax.fori_loop(0, groups, turn_edges, 0)
    keep_last(edge_two, rim_mixed)
    add_far_edges(1)
    if n_level > 1:
        end_hop(1, edge_two, 0, 0)

    for c in range(C):
        for s in range(S):
            left_own[c, s * Q : (s + 1) * Q, :] = beside(edge_one, spots[c][0][2], low_at, s)
    left_copies = [
        send(left_own, far_left.at[m], (far_left_send, far_left_recv), m, device)
        for m, device in enumerate(fars[:singles])
    ]

    combine(1, mixed, out_ref)
    if n_level > 1:
        end_hop(1, edge_two, 1, 0)

    def turn_mixed(h):
        def one(i, carry):
            for g in range(G):
                turned = turn(mixed, h, i, g)
                put(0, h, i, g, turned)
                for c in range(C):
                    at = (h * G + g) * HU
                    rim_two[c, i, :, at : at + HU] = turned[V - B :, c * HU : (c + 1) * HU]
            return carry

        lax.fori_loop(0, groups, one, 0, unroll=2)

    mixed_near = []
    for s in range(S):
        for copy in far_copies[s]:
            copy.wait_recv()
        add_far(s)
        fresh = []
        for r, device in enumerate(cores):
            index = (n_phase - 1) * (1 + s) + r
            fresh.append(send(mixed.at[:, s], near.at[1, r, :, s], near_sems, index, device))
        mixed_near += fresh
        if s == S - 1:
            turn_mixed(halves - 1)
        combine_far(s)
        for copy in fresh:
            copy.wait_recv()
        if (s + 1) % H == 0:
            if s < S - 1:
                turn_mixed(s // H)
            turn_near(1, [s // H])
        if s == max(0, S // 2 - 1):
            end_hops(1, edge_two, 1, 2)
    lax.fori_loop(1, V // B, multiply, 0)
    end_hops(1, edge_two, 2, n_level)
    last_picks = take_rims(1, edge_two, rim_two)
    pick_copies += last_picks
    add_above(edge_two)
    for copy in left_copies:
        copy.wait_recv()
    add_rows(1, edge_two, out_ref)
    share_rims(1, last_picks)
    multiply(0, 0)
    finish(1, out_ref)

    for copy in x_near + mixed_near + pick_copies + left_copies + edge_copies:
        copy.wait_send()
    for copies in far_copies:
        for copy in copies:
            copy.wait_send()
    end_sends(0, edge_one)
    end_sends(1, edge_two)


def body(
    n_level,
    n_phase,
    state_values,
    phase_rates,
    batch_rates,
    service_rates,
    source_rates,
    tile_levels,
    routes,
    tile_owner,
):
    C, S, Q, U, V = state_values.shape
    phases = phase_rates.shape[0]
    batch = batch_rates.shape[0]
    local_bits = S.bit_length() - 1
    cross = list(range(local_bits, SOURCES))
    masks = [1 << (k - local_bits) for k in cross]
    masks += [masks[i] | masks[j] for i in range(len(cross)) for j in range(i + 1, len(cross))]
    group = min(Q, max(1, 128 // (S * U)))
    lanes = group * S * U
    groups = Q // group
    halves = 2 if S > 1 else 1
    width = halves * (-(-(C * S * U // halves) // 128) * 128)
    edge_rows = groups * batch + 2 * C * S * Q + C * (-(-groups // 8) * 8)
    f32, bf16 = jnp.float32, jnp.bfloat16
    vmem = pl.BlockSpec(memory_space=pltpu.VMEM)
    singles, fars, cores = max(1, len(cross)), max(1, len(masks)), max(1, n_phase - 1)
    counts = [fars * S, singles, singles, cores * (1 + S), 2 * cores, max(1, 8 * (n_level - 1))]
    shapes = [
        ((fars,) + state_values.shape, f32),
        ((singles, edge_rows, lanes), f32),
        ((singles, C, S * Q, V), f32),
        ((2, cores) + state_values.shape, f32),
        (state_values.shape, f32),
        ((phases, batch + V, width), bf16),
        ((phases, batch + V, width), bf16),
        ((Q, V, width), f32),
        ((phases * 2 * batch, 128), f32),
        ((Q, batch, phases * 2 * batch), f32),
        ((2 * Q * batch, phases * 2 * batch), bf16),
        ((phases, V), f32),
        ((n_level, edge_rows, lanes), f32),
        ((n_level, edge_rows, lanes), f32),
        ((C, groups, batch, lanes), f32),
        ((C, groups, batch, lanes), f32),
        ((C, groups, batch, lanes), f32),
        ((2, n_phase, C, groups, batch, lanes), f32),
        ((C, S * Q, V), f32),
    ]
    operands = (
        service_rates,
        source_rates,
        tile_levels.T,
        routes,
        tile_owner,
        state_values,
        phase_rates,
        batch_rates,
    )
    return pl.pallas_call(
        functools.partial(kernel, (n_level, n_phase, masks, local_bits, cross)),
        out_shape=jax.ShapeDtypeStruct(state_values.shape, f32),
        in_specs=[pl.BlockSpec(memory_space=pl.ANY)] * 8,
        out_specs=vmem,
        scratch_shapes=[pltpu.SMEM(a.shape, a.dtype) for a in operands[:5]]
        + [pltpu.VMEM(a.shape, a.dtype) for a in operands[5:]]
        + [pltpu.SemaphoreType.DMA((len(operands),))]
        + [pltpu.VMEM(*shape) for shape in shapes]
        + [pltpu.SemaphoreType.DMA((n,)) for n in counts for _ in range(2)],
        compiler_params=pltpu.CompilerParams(
            collective_id=0, has_side_effects=True, vmem_limit_bytes=60 * 1024 * 1024
        ),
    )(*operands)


def solution(mesh):
    placed = (
        P(("groups", "level"), "src", "phase", None, None),
        P("groups", None),
        P("groups", None, None),
        P("groups"),
        P("groups", None),
        P("groups", None),
        P("groups", None),
        P("groups"),
    )
    axes = mesh.shape
    return jax.shard_map(
        functools.partial(body, axes["level"], axes["phase"]),
        mesh=mesh,
        in_specs=placed,
        out_specs=P(("groups", "level"), "src", "phase", None, None),
        check_vma=False,
    )
```
